128 devices in a mesh: group: 4 (over y_hi, core), fsdp: 32 (over z, y_lo, x).
Axes of the slice: x: 4, y: 4 (y_hi: 2, y_lo: 2; y = y_hi * 2 + y_lo), z: 4, core: 2. Of those that a mesh axis runs over, the one named last changes fastest.
Arguments:
- tokens: bfloat16 [65536, 7168], P(('group', 'fsdp')), may hold values from -6 to 6
- out_grad: bfloat16 [65536, 512], P(('group', 'fsdp')), may hold values from -6 to 6
- proj_weight: bfloat16 [7168, 512], P('fsdp'), may hold values from -0.0625 to 0.0625
- momentum: float32 [4, 896, 4096], P('group', 'fsdp'), may hold values from -6 to 6
- freq_index: int32 [4, 896, 32], P(None, 'fsdp'), may hold values from 0 to 4095, as said below
Outputs:
- latent: bfloat16 [65536, 512], P(('group', 'fsdp'))
- grad_in: bfloat16 [65536, 7168], P(('group', 'fsdp'))
- momentum_out: float32 [4, 896, 4096], P('group', 'fsdp')
- update: float32 [896, 4096], P('fsdp')
The draws below stay inside these ranges and needn't reach their ends.
Inputs may be any that keep to these rules, and one draw needn't show every extreme that they name: `freq_index`: for each replica and tile the 32 entries are distinct flattened frequencies (row frequency times 64 plus column frequency).
All inputs are finite; a program needn't handle non-finite values.
Results may differ from the reference program's by a relative error of at most 0.00055.
Values may be sent and summed in bfloat16 or wider, within the bound.
A program may use at most 192 MiB of HBM per device.

```python
import math
import jax
import jax.numpy as jnp
from jax import lax

D = 7168
KV = 512
TOK_DEV = 512
SIDE = 64
FREQS = 32
GROUPS = 4
TOKENS = 65536
TILES = 896
N_GROUP = 4
N_FSDP = 32


def draw_freq_index(key, part):
    key = jax.random.fold_in(key, 7)
    tile_cells = SIDE * SIDE
    position = jnp.arange(tile_cells, dtype=jnp.int32)
    scores = jax.random.randint(key, (GROUPS, TILES, tile_cells), 0, 2 ** 18, dtype=jnp.int32) * tile_cells + position
    forced = (jnp.arange(GROUPS)[:, None, None] == 0) & (jnp.arange(TILES)[None, :, None] == 0) & ((position == 0) | (position == tile_cells - 1))[None, None, :]
    scores = jnp.where(forced, 2 ** 30 + position, scores)
    return lax.top_k(scores, FREQS)[1].astype(jnp.int32)


def block_levels(rng, extent, pieces, smallest, largest):
    def one(axis_at, parts):
        steps = jax.random.uniform(jax.random.fold_in(jax.random.fold_in(rng, 6), axis_at), (parts,), jnp.float32, smallest / len(pieces), largest / len(pieces))
        return jnp.repeat(jnp.exp(steps), extent[axis_at] // parts).reshape((-1,) + (1,) * (len(extent) - axis_at - 1))

    level = one(*pieces[0])
    for cut in pieces[1:]:
        level = level * one(*cut)
    return level


def scatter_about(rng, dims, deviation, reach, split=(), kind=jnp.bfloat16):
    values = jax.random.normal(rng, dims, jnp.float32) * deviation
    if len(split) > 0:
        values = block_levels(rng, dims, split, -0.22, 0.18) * values
    return jnp.clip(values, min=-reach, max=reach).astype(kind)


def setup_inputs(seed: int = 0) -> dict:
    arg_keys = jax.random.split(jax.random.key(seed), 6)
    return {
        "tokens": scatter_about(arg_keys[0], (TOKENS, D), 1.0, 6.0, ((0, 128),)),
        "out_grad": scatter_about(arg_keys[1], (TOKENS, KV), 1.0, 6.0, ((0, 128),)),
        "proj_weight": scatter_about(arg_keys[2], (D, KV), D ** -0.5, 0.0625, ((0, 32),)),
        "momentum": scatter_about(arg_keys[3], (GROUPS, TILES, SIDE * SIDE), 1.0, 6.0, ((0, 4), (1, 32)), jnp.float32),
        "freq_index": draw_freq_index(jax.random.fold_in(arg_keys[5], 71), 0),
    }


decay_rate = 0.9
highest = lax.Precision.HIGHEST

def cosine_table():
    sample_index = jnp.arange(SIDE, dtype=jnp.float32)
    frequency = sample_index[:, None]
    scaling = jnp.where(frequency == 0, math.sqrt(1.0 / SIDE), math.sqrt(2.0 / SIDE))
    return scaling * jnp.cos(math.pi * (2.0 * sample_index[None, :] + 1.0) * frequency / (2.0 * SIDE))

def forward_transform(blocks, cosines):
    halfway = jnp.einsum('ik,ckl->cil', cosines, blocks, precision=highest)
    return jnp.einsum('cil,jl->cij', halfway, cosines, precision=highest)

def inverse_transform(coeffs, cosines):
    halfway = jnp.einsum('ki,ckl->cil', cosines, coeffs, precision=highest)
    return jnp.einsum('cil,lj->cij', halfway, cosines, precision=highest)

def to_tiles(matrix):
    shaped = matrix.reshape(D // SIDE, SIDE, KV // SIDE, SIDE).transpose(0, 2, 1, 3)
    return shaped.reshape(TILES, SIDE * SIDE)

def reference(tokens, out_grad, proj_weight, momentum, freq_index):
    latent = jnp.dot(tokens, proj_weight, preferred_element_type=jnp.float32).astype(jnp.bfloat16)
    grad_in = jnp.dot(out_grad, proj_weight.T, preferred_element_type=jnp.float32).astype(jnp.bfloat16)
    cosines = cosine_table()
    grad_scale = 1.0 / math.sqrt(TOK_DEV * N_FSDP)
    token_parts = tokens.reshape(N_GROUP, N_FSDP, TOK_DEV, D)
    grad_parts = out_grad.reshape(N_GROUP, N_FSDP, TOK_DEV, KV)
    tile_rows = jnp.arange(TILES, dtype=jnp.int32)[:, None]
    summed_picks = jnp.zeros((TILES, SIDE * SIDE), jnp.float32)
    leftovers = []

    def add_part(running, inputs_pair):
        partial_value = jnp.dot(inputs_pair[0].T, inputs_pair[1], preferred_element_type=jnp.float32)
        return (running + partial_value, None)
    for group_index in range(N_GROUP):
        summed, _ = lax.scan(add_part, jnp.zeros((D, KV), jnp.float32), (token_parts[group_index], grad_parts[group_index]))
        gradient = to_tiles(summed) * grad_scale
        accumulated = decay_rate * momentum[group_index] + gradient
        coeffs = forward_transform(accumulated.reshape(TILES, SIDE, SIDE), cosines).reshape(TILES, SIDE * SIDE)
        own_index = freq_index[group_index]
        picked = jnp.take_along_axis(coeffs, own_index, axis=1)
        own_sparse = jnp.zeros((TILES, SIDE * SIDE), jnp.float32).at[tile_rows, own_index].add(picked)
        removed = inverse_transform(own_sparse.reshape(TILES, SIDE, SIDE), cosines).reshape(TILES, SIDE * SIDE)
        leftovers.append(accumulated - removed)
        summed_picks = summed_picks + own_sparse
    averaged = (summed_picks / N_GROUP).reshape(TILES, SIDE, SIDE)
    update = inverse_transform(averaged, cosines).reshape(TILES, SIDE * SIDE)
    return (latent, grad_in, jnp.stack(leftovers), update)
```

```python
import functools
import math

import jax
import jax.numpy as jnp
import numpy as np
from jax import lax
from jax.experimental import pallas as pl
from jax.experimental.pallas import tpu as pltpu
from jax.sharding import PartitionSpec as P

SIDE = 64
HB = 7
DECAY = 0.9
MESH = pl.DeviceIdType.MESH
F32 = jnp.float32
BF16 = jnp.bfloat16
I16 = jnp.int16
TOK, WIDE, KV = 512, 7168, 512


def cosine_tables():
    n = np.arange(SIDE, dtype=np.float64)
    k = n[:, None]
    scale = np.where(k == 0, math.sqrt(1.0 / SIDE), math.sqrt(2.0 / SIDE))
    table = scale * np.cos(math.pi * (2.0 * n[None, :] + 1.0) * k / (2.0 * SIDE))
    t = table.T.astype(np.float32)
    high = t.astype(jnp.bfloat16)
    low = (t - high.astype(np.float32)).astype(jnp.bfloat16)
    return np.concatenate([high, low], axis=0)


def rem4(v):
    return lax.rem(v + 4, 4)


def dot(a, b):
    return jnp.dot(a, b, preferred_element_type=F32)


def dot_nt(a, b):
    return lax.dot_general(a, b, (((1,), (1,)), ((), ())), preferred_element_type=F32)


def split(v):
    high = v.astype(BF16)
    return high, (v - high.astype(F32)).astype(BF16)


def quantize(v, q_ref, s_ref, row):
    a = jnp.max(jnp.max(jnp.abs(v), axis=0), axis=0, keepdims=True)
    m = jnp.maximum(jnp.maximum(a[:, :128], a[:, 128:]), 1e-30)
    s = m * (1.0 / 32760.0)
    inv = 1.0 / s
    inv2 = jnp.concatenate([inv, inv], axis=1)[None]
    q_ref[...] = jnp.round(v * inv2).astype(jnp.int32).astype(I16)
    s_ref[pl.ds(row, 1), :] = s


def dequantize(q_ref, s_ref, row):
    s = s_ref[pl.ds(row, 1), :]
    s2 = jnp.concatenate([s, s], axis=1)[None]
    return q_ref[...].astype(jnp.int32).astype(F32) * s2


def kernel(
    grad_scale,
    tok_ref, og_ref, w_ref, mom_ref, freq_ref, ct_ref,
    w_out, mom_out, upd_out,
    T, TT, O, W, tmp, SQ, SS, RQ, RS, GH, GO, YQ, YS, ZQ, ZS, TQ, TS, VQ, VS, VH, VL, U, PA,
    load_sem, w_sem, ag_send, ag_recv, core_send, core_recv,
    m_send, m_recv, y_send, y_recv, t_send, t_recv, p_send, p_recv,
):
    g = lax.axis_index("group")
    f = lax.axis_index("fsdp")
    c = lax.rem(g, 2)
    yh = lax.div(g, 2)
    z, yl, x = lax.div(f, 8), lax.rem(lax.div(f, 4), 2), lax.rem(f, 4)
    p0 = x * (1 - c) + z * c
    s0 = z * (1 - c) + x * c

    def f_of(p, s, y):
        xx = p * (1 - c) + s * c
        zz = s * (1 - c) + p * c
        return zz * 8 + y * 4 + xx

    def at_ps(dp, ds):
        return (g, f_of(rem4(p0 + dp), rem4(s0 + ds), yl))

    def at_y(dy):
        yy = rem4(yh * 2 + yl + dy)
        return (lax.div(yy, 2) * 2 + c, f_of(p0, s0, lax.rem(yy, 2)))

    sib = (yh * 2 + 1 - c, f)
    far = ((1 - yh) * 2 + c, f)
    far_sib = ((1 - yh) * 2 + 1 - c, f)
    pn = (at_ps(1, 0), at_ps(-1, 0))
    sn = (at_ps(0, 1), at_ps(0, -1))
    yn = (at_y(1), at_y(-1))
    y_pair = (g, f_of(p0, s0, 1 - yl))

    og_load = pltpu.make_async_copy(og_ref, O, load_sem.at[8])
    og_load.start()
    tok_loads = []
    for i in range(8):
        cp = pltpu.make_async_copy(
            tok_ref.at[:, pl.ds(896 * i, 896)], T.at[:, pl.ds(896 * i, 896)], load_sem.at[i]
        )
        cp.start()
        tok_loads.append(cp)
    w_load = pltpu.make_async_copy(w_ref, W.at[f], w_sem.at[0])
    w_load.start()

    barrier = pltpu.get_barrier_semaphore()
    for d in (*pn, *sn, *yn, sib, far, far_sib):
        pl.semaphore_signal(barrier, inc=1, device_id=d, device_id_type=MESH)
    pl.semaphore_wait(barrier, 9)

    sends = []

    def remote(src, dst, ss, rs, dev):
        cp = pltpu.make_async_remote_copy(
            src_ref=src, dst_ref=dst, send_sem=ss, recv_sem=rs, device_id=dev, device_id_type=MESH
        )
        cp.start()
        sends.append(cp)
        return cp

    def fb(j, t):
        return f_of(rem4(p0 + j), rem4(s0 + t), yl)

    def block(fi):
        return W.at[fi, c]

    n_core = [0]
    core_copies = []

    def to_core(fi):
        i = n_core[0]
        n_core[0] += 1
        core_copies.append(remote(block(fi), block(fi), core_send.at[i], core_recv.at[i], sib))

    w_load.wait()
    n_ag = [0]

    def ag(fi, dev):
        i = n_ag[0]
        n_ag[0] += 1
        return remote(block(fi), block(fi), ag_send.at[i], ag_recv.at[i], dev)

    def s_out(j, t):
        return ag(fb(j, t), yn[0] if j in (0, 1) else yn[1])

    a_p = [ag(fb(0, 0), pn[0]), ag(fb(0, 0), pn[1])]
    a_s = {}
    for d in range(2):
        a_s[d, 0] = ag(fb(0, 0), sn[d])
    a_y = [s_out(0, 0)]

    def ag2():
        a_p[0].wait_recv()
        a_p[1].wait_recv()
        a_p.append(ag(fb(3, 0), pn[0]))
        for j in (3, 1):
            for d in range(2):
                a_s[d, j] = ag(fb(j, 0), sn[d])
        for j in (3, 1):
            a_y.append(s_out(j, 0))
            to_core(fb(j, 0))

    def ag3():
        a_p[2].wait_recv()
        for d in range(2):
            a_s[d, 2] = ag(fb(2, 0), sn[d])
        a_y.append(s_out(2, 0))
        to_core(fb(2, 0))

    a_f = []

    def ag4():
        for j in (0, 3, 1, 2):
            for d in range(2):
                a_s[d, j].wait_recv()
        for j in (0, 1):
            a_f.append(ag(fb(j, 3), sn[0]))
        for j in (2, 3):
            a_f.append(ag(fb(j, 1), sn[1]))
        for t in (3, 1):
            for j in range(4):
                a_y.append(s_out(j, t))
                to_core(fb(j, t))

    def ag5():
        for cp in a_f:
            cp.wait_recv()
        for j in range(4):
            a_y.append(s_out(j, 2))
            to_core(fb(j, 2))

    def ag6():
        for cp in a_y:
            cp.wait_recv()
        for j in range(4):
            for t in range(4):
                to_core(f_of(rem4(p0 + j), rem4(s0 + t), 1 - yl))

    def ag7():
        for cp in core_copies:
            cp.wait_recv()

    def transpose(i):
        tok_loads[i].wait()

        @pl.loop(0, 7)
        def _(b):
            col = pl.multiple_of(i * 896 + b * 128, 128)
            TT[pl.ds(col, 128), :] = T[:, pl.ds(col, 128)].T

    def s_off(k):
        return lax.rem(2 + 3 * k + lax.div(k, 2) * (3 - 2 * lax.rem(k, 2)), 4)

    def chunk(dp, k, y):
        fi = f_of(rem4(p0 + dp), rem4(s0 + s_off(k)), y)
        e = lax.rem(fi, 2)
        row = pl.multiple_of(64 * (7 * lax.div(fi, 2) + 3 * e), 64)
        res = dot(TT[pl.ds(row, 256), :], O[...])
        for i in range(4):
            for h in range(2):
                tmp[y, 2 * i + h] = res[64 * i : 64 * i + 64, 256 * h : 256 * h + 256]
        return e

    def half(h):
        return pl.ds(32 * h, 32)

    def send_m(m, d, k):
        def one(src, dst, i):
            pltpu.make_async_remote_copy(
                src_ref=src.at[m, d, k], dst_ref=dst.at[m, d, k], send_sem=m_send.at[m, d, k, i],
                recv_sem=m_recv.at[m, d, k, i], device_id=pn[d], device_id_type=MESH,
            ).start()

        one(SQ, RQ, 0)
        one(SS, RS, 1)

    def copy_m(m, d, k, i):
        src, dst = ((SQ, RQ), (SS, RS))[i]
        return pltpu.make_async_remote_copy(
            src_ref=src.at[m, d, k], dst_ref=dst.at[m, d, k], send_sem=m_send.at[m, d, k, i],
            recv_sem=m_recv.at[m, d, k, i], device_id=pn[d], device_id_type=MESH,
        )

    def recv_m(m, d, k):
        copy_m(m, d, k, 0).wait_recv()
        copy_m(m, d, k, 1).wait_recv()

    def prepare(i):
        fr = freq_ref[i]
        iota = lax.broadcasted_iota(jnp.int32, (64, 128), 0)
        eu = (iota == lax.shift_right_logical(fr, 6)).astype(F32).astype(BF16)
        ev = (iota == (fr & 63)).astype(F32).astype(BF16)
        res = dot(ct_ref[...], jnp.concatenate([eu, ev], axis=1))
        U[i] = res[:64, :128] + res[64:, :128]
        lane = lax.broadcasted_iota(jnp.int32, (64, 128), 1)
        for t in range(4):
            mine = lax.shift_right_logical(lane, 5) == t
            VH[i, 64 * t : 64 * t + 64, :] = jnp.where(mine, res[:64, 128:], 0.0).astype(BF16)
            VL[i, 64 * t : 64 * t + 64, :] = jnp.where(mine, res[64:, 128:], 0.0).astype(BF16)

    for i in range(4):
        transpose(i)
    ag2()
    for i in range(4, 8):
        transpose(i)
    ag3()
    og_load.wait()

    def first(k):
        for y in range(2):
            e = chunk(2, k, y)
            for d in range(2):
                quantize(tmp[y, pl.ds(e, 7), half(d), :], SQ.at[0, d, k, y], SS.at[0, d, k], y)
        for d in range(2):
            send_m(0, d, k)

    pl.loop(0, 2)(first)
    ag4()
    pl.loop(2, 4)(first)
    ag5()

    @pl.loop(0, 4)
    def _(k):
        for d in range(2):
            for y in range(2):
                e = chunk(1 if d == 0 else -1, k, y)
                quantize(tmp[y, pl.ds(e, 7), half(1 - d), :], SQ.at[1, d, k, y], SS.at[1, d, k], y)
                GH[d, k, y] = tmp[y, pl.ds(e, 7), half(d), :]
            send_m(1, d, k)

    @pl.loop(0, 4)
    def _(k):
        for d in range(2):
            recv_m(0, d, k)
            for y in range(2):
                v = GH[d, k, y] + dequantize(RQ.at[0, d, k, y], RS.at[0, d, k], y)
                quantize(v, SQ.at[2, d, k, y], SS.at[2, d, k], y)
            send_m(2, d, k)

    @pl.loop(0, 4)
    def _(k):
        for y in range(2):
            e = chunk(0, k, y)
            GO[k, y] = tmp[y, pl.ds(e, 7)]

    ag6()
    pl.loop(0, 28)(prepare)

    def y_copy(k, i):
        src, dst = ((YQ, ZQ), (YS, ZS))[i]
        return pltpu.make_async_remote_copy(
            src_ref=src.at[k], dst_ref=dst.at[k], send_sem=y_send.at[k, i],
            recv_sem=y_recv.at[k, i], device_id=y_pair, device_id_type=MESH,
        )

    def sum_p(k):
        for d in range(2):
            recv_m(1, d, k)
            recv_m(2, d, k)

        def total(y, d):
            return (
                GO[k, y, :, half(d), :]
                + dequantize(RQ.at[2, d, k, y], RS.at[2, d, k], y)
                + dequantize(RQ.at[1, 1 - d, k, y], RS.at[1, 1 - d, k], y)
            )

        for d in range(2):
            quantize(total(1 - yl, d), YQ.at[k, d], YS.at[k], d)
        y_copy(k, 0).start()
        y_copy(k, 1).start()
        for d in range(2):
            GO[k, 0, :, half(d), :] = total(yl, d)

    def t_copy(m, d, i):
        src, dst = ((TQ, VQ), (TS, VS))[i]
        return pltpu.make_async_remote_copy(
            src_ref=src.at[m, d], dst_ref=dst.at[m, d], send_sem=t_send.at[m, d, i],
            recv_sem=t_recv.at[m, d, i], device_id=sn[d], device_id_type=MESH,
        )

    def sum_y(k):
        y_copy(k, 0).wait_recv()
        y_copy(k, 1).wait_recv()
        return [
            GO[k, 0, :, half(d), :] + dequantize(ZQ.at[k, d], ZS.at[k], d) for d in range(2)
        ]

    def send_t(m, d, v):
        quantize(v, TQ.at[m, d], TS.at[m, d], 0)
        t_copy(m, d, 0).start()
        t_copy(m, d, 1).start()

    def recv_t(m, d):
        t_copy(m, d, 0).wait_recv()
        t_copy(m, d, 1).wait_recv()
        return dequantize(VQ.at[m, d], VS.at[m, d], 0)

    sum_p(0)
    sum_p(1)
    a = sum_y(0)
    for d in range(2):
        send_t(0, d, a[d])
    sum_p(2)
    a = sum_y(1)
    send_t(1, 0, a[1])
    GO[1, 0, :, half(0), :] = a[0]
    sum_p(3)
    send_t(2, 0, GO[1, 0, :, half(0), :] + recv_t(0, 0))
    a = sum_y(2)
    send_t(1, 1, a[0])
    send_t(2, 1, a[1] + recv_t(0, 1))
    ag7()
    w_store = pltpu.make_async_copy(W, w_out, w_sem.at[1])
    w_store.start()
    a = sum_y(3)
    for d in range(2):
        v = a[d] + recv_t(2, d) + recv_t(1, 1 - d)
        GO[0, 0, :, half(d), :] = v * grad_scale + DECAY * mom_ref[:, half(d), :]

    own = g * HB

    @pl.loop(0, HB)
    def _(i):
        xh, xl = split(GO[0, 0, i])
        r = dot(xh, VH[own + i]) + dot(xl, VH[own + i]) + dot(xh, VL[own + i])
        PA[g, i] = jnp.sum(U[own + i] * r, axis=0, keepdims=True)

    peers = (sib, far, far_sib)
    p_copies = [
        pltpu.make_async_remote_copy(
            src_ref=PA.at[g], dst_ref=PA.at[g], send_sem=p_send.at[i], recv_sem=p_recv.at[i],
            device_id=d, device_id_type=MESH,
        )
        for i, d in enumerate(peers)
    ]
    for cp in p_copies:
        cp.start()

    def back(j, i):
        uh, ul = split(U[j * HB + i] * PA[j, i])
        vh, vl = VH[j * HB + i], VL[j * HB + i]
        return dot_nt(uh, vh) + dot_nt(ul, vh) + dot_nt(uh, vl)

    @pl.loop(0, HB)
    def _(i):
        mom_out[i] = GO[0, 0, i] - back(g, i)

    for cp in p_copies:
        cp.wait_recv()

    @pl.loop(0, HB)
    def _(i):
        upd_out[i] = 0.25 * ((back(0, i) + back(1, i)) + (back(2, i) + back(3, i)))

    for cp in p_copies:
        cp.wait_send()
    for cp in sends:
        cp.wait_send()

    @pl.loop(0, 4)
    def _(k):
        for m in range(3):
            for d in range(2):
                copy_m(m, d, k, 0).wait_send()
                copy_m(m, d, k, 1).wait_send()
        y_copy(k, 0).wait_send()
        y_copy(k, 1).wait_send()

    for m in range(3):
        for d in range(2):
            t_copy(m, d, 0).wait_send()
            t_copy(m, d, 1).wait_send()
    w_store.wait()


def on_device(tokens, out_grad, proj_weight, momentum, freq_index):
    grad_scale = 1.0 / math.sqrt(TOK * 32)
    mom = momentum[0].reshape(HB, 4, SIDE, SIDE).transpose(0, 2, 1, 3).reshape(HB, SIDE, 256)
    freq = freq_index.reshape(4 * HB, 1, 128)
    any_spec = pl.BlockSpec(memory_space=pl.ANY)
    vmem = pl.BlockSpec(memory_space=pltpu.VMEM)
    dma = pltpu.SemaphoreType.DMA
    full, mom_out, upd = pl.pallas_call(
        functools.partial(kernel, grad_scale),
        out_shape=(
            jax.ShapeDtypeStruct((32, 2, 112, KV), BF16),
            jax.ShapeDtypeStruct((HB, SIDE, 256), F32),
            jax.ShapeDtypeStruct((HB, SIDE, 256), F32),
        ),
        in_specs=[any_spec, any_spec, any_spec, vmem, vmem, vmem],
        out_specs=(any_spec, vmem, vmem),
        scratch_shapes=[
            pltpu.VMEM((TOK, WIDE), BF16),
            pltpu.VMEM((WIDE, TOK), BF16),
            pltpu.VMEM((TOK, KV), BF16),
            pltpu.VMEM((32, 2, 112, KV), BF16),
            pltpu.VMEM((2, 8, 64, 256), F32),
            pltpu.VMEM((3, 2, 4, 2, HB, 32, 256), I16),
            pltpu.VMEM((3, 2, 4, 2, 128), F32),
            pltpu.VMEM((3, 2, 4, 2, HB, 32, 256), I16),
            pltpu.VMEM((3, 2, 4, 2, 128), F32),
            pltpu.VMEM((2, 4, 2, HB, 32, 256), F32),
            pltpu.VMEM((4, 2, HB, 64, 256), F32),
            pltpu.VMEM((4, 2, HB, 32, 256), I16),
            pltpu.VMEM((4, 2, 128), F32),
            pltpu.VMEM((4, 2, HB, 32, 256), I16),
            pltpu.VMEM((4, 2, 128), F32),
            pltpu.VMEM((3, 2, HB, 32, 256), I16),
            pltpu.VMEM((3, 2, 1, 128), F32),
            pltpu.VMEM((3, 2, HB, 32, 256), I16),
            pltpu.VMEM((3, 2, 1, 128), F32),
            pltpu.VMEM((4 * HB, 256, 128), BF16),
            pltpu.VMEM((4 * HB, 256, 128), BF16),
            pltpu.VMEM((4 * HB, 64, 128), F32),
            pltpu.VMEM((4, HB, 1, 128), F32),
            dma((9,)),
            dma((2,)),
            dma((40,)),
            dma((40,)),
            dma((31,)),
            dma((31,)),
            dma((3, 2, 4, 2)),
            dma((3, 2, 4, 2)),
            dma((4, 2)),
            dma((4, 2)),
            dma((3, 2, 2)),
            dma((3, 2, 2)),
            dma((3,)),
            dma((3,)),
        ],
        compiler_params=pltpu.CompilerParams(
            collective_id=0, has_side_effects=True, vmem_limit_bytes=62 << 20
        ),
        cost_estimate=pl.CostEstimate(
            flops=4 * 10**9, bytes_accessed=24 * 10**6, transcendentals=0
        ),
    )(tokens, out_grad, proj_weight.reshape(2, 112, KV), mom, freq, jnp.asarray(cosine_tables()))
    full = full.reshape(WIDE, KV)
    latent = dot(tokens, full).astype(BF16)
    grad_in = dot_nt(out_grad, full).astype(BF16)

    def to_tiles(v):
        return v.reshape(HB, SIDE, 4, SIDE).transpose(0, 2, 1, 3).reshape(4 * HB, SIDE * SIDE)

    return latent, grad_in, to_tiles(mom_out)[None], to_tiles(upd)


def solution(mesh):
    return jax.shard_map(
        on_device,
        mesh=mesh,
        in_specs=(
            P(("group", "fsdp"), None),
            P(("group", "fsdp"), None),
            P("fsdp", None),
            P("group", "fsdp", None),
            P(None, "fsdp", None),
        ),
        out_specs=(
            P(("group", "fsdp"), None),
            P(("group", "fsdp"), None),
            P("group", "fsdp", None),
            P("fsdp", None),
        ),
        check_vma=False,
    )
```

```python
import functools
import math

import jax
import jax.numpy as jnp
import numpy as np
from jax import lax
from jax.experimental import pallas as pl
from jax.experimental.pallas import tpu as pltpu
from jax.sharding import PartitionSpec as P

SIDE = 64
HB = 7
DECAY = 0.9
MESH = pl.DeviceIdType.MESH
F32 = jnp.float32
BF16 = jnp.bfloat16
I16 = jnp.int16
TOK, WIDE, KV = 512, 7168, 512


def cosine_tables():
    n = np.arange(SIDE, dtype=np.float64)
    k = n[:, None]
    scale = np.where(k == 0, math.sqrt(1.0 / SIDE), math.sqrt(2.0 / SIDE))
    table = scale * np.cos(math.pi * (2.0 * n[None, :] + 1.0) * k / (2.0 * SIDE))
    t = table.T.astype(np.float32)
    high = t.astype(jnp.bfloat16)
    low = (t - high.astype(np.float32)).astype(jnp.bfloat16)
    return np.concatenate([high, low], axis=0)


def rem4(v):
    return lax.rem(v + 4, 4)


def dot(a, b):
    return jnp.dot(a, b, preferred_element_type=F32)


def dot_nt(a, b):
    return lax.dot_general(a, b, (((1,), (1,)), ((), ())), preferred_element_type=F32)


def split(v):
    high = v.astype(BF16)
    return high, (v - high.astype(F32)).astype(BF16)


def quantize(v, q_ref, s_ref, row):
    a = jnp.max(jnp.max(jnp.abs(v), axis=0), axis=0, keepdims=True)
    m = jnp.maximum(jnp.maximum(a[:, :128], a[:, 128:]), 1e-30)
    s = m * (1.0 / 32760.0)
    inv = 1.0 / s
    inv2 = jnp.concatenate([inv, inv], axis=1)[None]
    q_ref[...] = jnp.round(v * inv2).astype(jnp.int32).astype(I16)
    s_ref[pl.ds(row, 1), :] = s


def dequantize(q_ref, s_ref, row):
    s = s_ref[pl.ds(row, 1), :]
    s2 = jnp.concatenate([s, s], axis=1)[None]
    return q_ref[...].astype(jnp.int32).astype(F32) * s2


def lane_low(shape):
    return lax.broadcasted_iota(jnp.int32, shape, len(shape) - 1) < 64


def kernel(
    grad_scale,
    tok_ref, og_ref, w_ref, mom_ref, freq_ref, ct_ref,
    w_out, mom_out, upd_out, lat_out,
    T, TT, O, W, tmp, SQ, SS, RQ, RS, GH, GO, YQ, YS, ZQ, ZS, TQ, TS, VQ, VS, VH, VL, U, PA, MP, MH, FR, LAT,
    load_sem, w_sem, ag_send, ag_recv, core_send, core_recv,
    m_send, m_recv, y_send, y_recv, t_send, t_recv, p_send, p_recv,
):
    g = lax.axis_index("group")
    f = lax.axis_index("fsdp")
    c = lax.rem(g, 2)
    yh = lax.div(g, 2)
    z, yl, x = lax.div(f, 8), lax.rem(lax.div(f, 4), 2), lax.rem(f, 4)
    p0 = x * (1 - c) + z * c
    s0 = z * (1 - c) + x * c

    def f_of(p, s, y):
        xx = p * (1 - c) + s * c
        zz = s * (1 - c) + p * c
        return zz * 8 + y * 4 + xx

    def at_ps(dp, ds):
        return (g, f_of(rem4(p0 + dp), rem4(s0 + ds), yl))

    def at_y(dy):
        yy = rem4(yh * 2 + yl + dy)
        return (lax.div(yy, 2) * 2 + c, f_of(p0, s0, lax.rem(yy, 2)))

    sib = (yh * 2 + 1 - c, f)
    far = ((1 - yh) * 2 + c, f)
    far_sib = ((1 - yh) * 2 + 1 - c, f)
    pn = (at_ps(1, 0), at_ps(-1, 0))
    sn = (at_ps(0, 1), at_ps(0, -1))
    yn = (at_y(1), at_y(-1))
    y_pair = (g, f_of(p0, s0, 1 - yl))

    barrier = pltpu.get_barrier_semaphore()
    for d in (*pn, *sn, *yn, sib, far, far_sib):
        pl.semaphore_signal(barrier, inc=1, device_id=d, device_id_type=MESH)

    S_OFF = (2, 1, 3, 0)

    og_load = pltpu.make_async_copy(og_ref, O, load_sem.at[8])
    og_load.start()
    w_load = pltpu.make_async_copy(w_ref, W.at[f], w_sem.at[0])
    w_load.start()
    tok_loads = []
    for i in range(4):
        for y in range(2):
            quad = rem4(z + S_OFF[i]) * 2 + y
            cols = pl.ds(pl.multiple_of(896 * quad, 128), 896)
            cp = pltpu.make_async_copy(tok_ref.at[:, cols], T.at[:, cols], load_sem.at[2 * i + y])
            cp.start()
            tok_loads.append(cp)
    mom_load = pltpu.make_async_copy(mom_ref, MP, w_sem.at[2])
    mom_load.start()
    freq_load = pltpu.make_async_copy(freq_ref, FR, w_sem.at[3])
    freq_load.start()

    sends = []

    def remote(src, dst, ss, rs, dev):
        cp = pltpu.make_async_remote_copy(
            src_ref=src, dst_ref=dst, send_sem=ss, recv_sem=rs, device_id=dev, device_id_type=MESH
        )
        cp.start()
        sends.append(cp)
        return cp

    def fb(j, t):
        return f_of(rem4(p0 + j), rem4(s0 + t), yl)

    def block(fi):
        return W.at[fi, c]

    core_copies = []

    def to_core(fi):
        i = len(core_copies)
        core_copies.append(remote(block(fi), block(fi), core_send.at[i], core_recv.at[i], sib))

    n_ag = [0]

    def ag(fi, dev):
        i = n_ag[0]
        n_ag[0] += 1
        return remote(block(fi), block(fi), ag_send.at[i], ag_recv.at[i], dev)

    def s_out(j, t):
        return ag(fb(j, t), yn[0] if j in (0, 1) else yn[1])

    a_p, a_s, a_y, a_f = [], {}, [], []

    def ag1():
        w_load.wait()
        for d in range(2):
            a_p.append(ag(fb(0, 0), pn[d]))
        for d in range(2):
            a_s[d, 0] = ag(fb(0, 0), sn[d])
        a_y.append(s_out(0, 0))

    def ag2():
        a_p[0].wait_recv()
        a_p[1].wait_recv()
        a_p.append(ag(fb(3, 0), pn[0]))
        for j in (3, 1):
            for d in range(2):
                a_s[d, j] = ag(fb(j, 0), sn[d])
        for j in (3, 1):
            a_y.append(s_out(j, 0))
            to_core(fb(j, 0))

    def ag3():
        a_p[2].wait_recv()
        for d in range(2):
            a_s[d, 2] = ag(fb(2, 0), sn[d])
        a_y.append(s_out(2, 0))
        to_core(fb(2, 0))

    def ag4():
        for j in (0, 3, 1, 2):
            for d in range(2):
                a_s[d, j].wait_recv()
        for j in (0, 1):
            a_f.append(ag(fb(j, 3), sn[0]))
        for j in (2, 3):
            a_f.append(ag(fb(j, 1), sn[1]))
        for t in (3, 1):
            for j in range(4):
                a_y.append(s_out(j, t))
                to_core(fb(j, t))

    def ag5():
        for cp in a_f:
            cp.wait_recv()
        for j in range(4):
            a_y.append(s_out(j, 2))
            to_core(fb(j, 2))

    def ag6(first):
        for cp in a_y[:12] if first else a_y[12:]:
            cp.wait_recv()
        for t in (0, 3, 1) if first else (2,):
            for j in range(4):
                to_core(f_of(rem4(p0 + j), rem4(s0 + t), 1 - yl))

    def ag7(low, high):
        for cp in core_copies[low:high]:
            cp.wait_recv()

    def latent_part(y, fresh):
        @pl.loop(0, 4)
        def _(i):
            cols = pl.ds(pl.multiple_of(896 * (2 * i + y), 128), 896)
            w = W[pl.ds(8 * i + 4 * y, 4)].reshape(896, KV)
            part = dot(T[:, cols], w)
            if fresh:

                @pl.when(i == 0)
                def _():
                    LAT[...] = part

                @pl.when(i > 0)
                def _():
                    LAT[...] += part
            else:
                LAT[...] += part

    def transpose(i):
        for y in range(2):
            tok_loads[2 * i + y].wait()
            quad = rem4(z + S_OFF[i]) * 2 + y

            @pl.loop(0, 7)
            def _(b):
                col = pl.multiple_of(quad * 896 + b * 128, 128)
                TT[pl.ds(col, 128), :] = T[:, pl.ds(col, 128)].T

    def chunk(dp, k, y, slot):
        fi = f_of(rem4(p0 + dp), rem4(s0 + S_OFF[k]), y)
        e = lax.rem(fi, 2)
        row = pl.multiple_of(64 * (7 * lax.div(fi, 2) + 3 * e), 64)
        res = dot(TT[pl.ds(row, 256), :], O[...])
        for i in range(4):
            for h in range(2):
                tmp[slot, 2 * i + h] = res[64 * i : 64 * i + 64, 256 * h : 256 * h + 256]
        return e

    def half(h):
        return pl.ds(32 * h, 32)

    def copy_m(m, d, k, i):
        src, dst = ((SQ, RQ), (SS, RS))[i]
        return pltpu.make_async_remote_copy(
            src_ref=src.at[m, d, k], dst_ref=dst.at[m, d, k], send_sem=m_send.at[m, d, k, i],
            recv_sem=m_recv.at[m, d, k, i], device_id=pn[d], device_id_type=MESH,
        )

    def send_m(m, d, k):
        copy_m(m, d, k, 0).start()
        copy_m(m, d, k, 1).start()

    def recv_m(m, d, k):
        copy_m(m, d, k, 0).wait_recv()
        copy_m(m, d, k, 1).wait_recv()

    def prepare(i):
        fr4 = jnp.concatenate([FR[4 * i + t] for t in range(4)], axis=1)
        for j in range(4):
            fr = fr4[j : j + 1, :]
            iota = lax.broadcasted_iota(jnp.int32, (64, 128), 0)
            eu = (iota == lax.shift_right_logical(fr, 6)).astype(F32).astype(BF16)
            ev = (iota == (fr & 63)).astype(F32).astype(BF16)
            res = dot(ct_ref[...], jnp.concatenate([eu, ev], axis=1))
            U[j * HB + i] = res[:64, :128] + res[64:, :128]
            lane = lax.broadcasted_iota(jnp.int32, (64, 128), 1)
            for t in range(4):
                mine = lax.shift_right_logical(lane, 5) == t
                rows = slice(64 * t, 64 * t + 64)
                VH[j * HB + i, rows, :] = jnp.where(mine, res[:64, 128:], 0.0).astype(BF16)
                VL[j * HB + i, rows, :] = jnp.where(mine, res[64:, 128:], 0.0).astype(BF16)

    def unpack_momentum():
        mom_load.wait()
        low = lane_low((32, 128))

        @pl.loop(0, HB)
        def _(i):
            for v in range(2):
                a, b = MP[4 * i + 2 * v], MP[4 * i + 2 * v + 1]
                MH[i, v, pl.ds(0, 32, stride=2), :] = DECAY * jnp.where(low, a, pltpu.roll(b, 64, 1))
                MH[i, v, pl.ds(1, 32, stride=2), :] = DECAY * jnp.where(low, pltpu.roll(a, 64, 1), b)

    def first(k):
        for y in range(2):
            e = chunk(2, k, y, y)
            for d in range(2):
                quantize(tmp[y, pl.ds(e, 7), half(d), :], SQ.at[0, d, k, y], SS.at[0, d, k], y)

    def second(k):
        for d in range(2):
            for y in range(2):
                slot = 2 * d + y
                e = chunk(1 if d == 0 else -1, k, y, slot)
                quantize(
                    tmp[slot, pl.ds(e, 7), half(1 - d), :], SQ.at[1, d, k, y], SS.at[1, d, k], y
                )
                GH[d, k, y] = tmp[slot, pl.ds(e, 7), half(d), :]
            send_m(1, d, k)

    def third(k):
        for d in range(2):
            recv_m(0, d, k)
            for y in range(2):
                v = GH[d, k, y] + dequantize(RQ.at[0, d, k, y], RS.at[0, d, k], y)
                quantize(v, SQ.at[2, d, k, y], SS.at[2, d, k], y)
            send_m(2, d, k)

    def own_part(k):
        for y in range(2):
            e = chunk(0, k, y, y)
            GO[k, y] = tmp[y, pl.ds(e, 7)]

    def y_copy(k, i):
        src, dst = ((YQ, ZQ), (YS, ZS))[i]
        return pltpu.make_async_remote_copy(
            src_ref=src.at[k], dst_ref=dst.at[k], send_sem=y_send.at[k, i],
            recv_sem=y_recv.at[k, i], device_id=y_pair, device_id_type=MESH,
        )

    def sum_p(k):
        for d in range(2):
            recv_m(1, d, k)
            recv_m(2, d, k)

        def total(y, d):
            return (
                GO[k, y, :, half(d), :]
                + dequantize(RQ.at[2, d, k, y], RS.at[2, d, k], y)
                + dequantize(RQ.at[1, 1 - d, k, y], RS.at[1, 1 - d, k], y)
            )

        for d in range(2):
            quantize(total(1 - yl, d), YQ.at[k, d], YS.at[k], d)
        y_copy(k, 0).start()
        y_copy(k, 1).start()
        for d in range(2):
            GO[k, 0, :, half(d), :] = total(yl, d)

    def t_copy(m, d, i):
        src, dst = ((TQ, VQ), (TS, VS))[i]
        return pltpu.make_async_remote_copy(
            src_ref=src.at[m, d], dst_ref=dst.at[m, d], send_sem=t_send.at[m, d, i],
            recv_sem=t_recv.at[m, d, i], device_id=sn[d], device_id_type=MESH,
        )

    def sum_y(k):
        y_copy(k, 0).wait_recv()
        y_copy(k, 1).wait_recv()
        return [
            GO[k, 0, :, half(d), :] + dequantize(ZQ.at[k, d], ZS.at[k], d) for d in range(2)
        ]

    def send_t(m, d, v):
        quantize(v, TQ.at[m, d], TS.at[m, d], 0)
        t_copy(m, d, 0).start()
        t_copy(m, d, 1).start()

    def recv_t(m, d):
        t_copy(m, d, 0).wait_recv()
        t_copy(m, d, 1).wait_recv()
        return dequantize(VQ.at[m, d], VS.at[m, d], 0)

    def send_first(k):
        for d in range(2):
            send_m(0, d, k)

    transpose(0)
    og_load.wait()
    first(0)
    transpose(1)
    first(1)
    pl.semaphore_wait(barrier, 9)
    ag1()
    send_first(0)
    send_first(1)
    transpose(2)
    first(2)
    send_first(2)
    transpose(3)
    first(3)
    send_first(3)
    freq_load.wait()
    second(0)
    ag2()
    second(1)
    third(0)
    own_part(0)
    pl.loop(0, 2)(prepare)
    ag3()
    ag4()
    second(2)
    third(1)
    own_part(1)
    pl.loop(2, 4)(prepare)
    second(3)
    third(2)
    ag5()
    sum_p(0)
    own_part(2)
    pl.loop(4, HB)(prepare)
    third(3)
    own_part(3)
    unpack_momentum()
    sum_p(1)
    a = sum_y(0)
    for d in range(2):
        send_t(0, d, a[d])
    ag6(True)
    ag7(0, 15)
    latent_part(yl, True)
    sum_p(2)
    a = sum_y(1)
    send_t(1, 0, a[1])
    send_t(2, 0, a[0] + recv_t(0, 0))
    ag6(False)
    sum_p(3)
    a = sum_y(2)
    send_t(1, 1, a[0])
    send_t(2, 1, a[1] + recv_t(0, 1))
    ag7(15, 31)
    w_store = pltpu.make_async_copy(W, w_out, w_sem.at[1])
    w_store.start()
    latent_part(1 - yl, False)
    a = sum_y(3)
    for d in range(2):
        v = a[d] + recv_t(2, d) + recv_t(1, 1 - d)
        for h in range(2):
            cols = slice(128 * h, 128 * h + 128)
            GO[0, 0, :, half(d), cols] = v[:, :, cols] * grad_scale + MH[:, h, half(d), :]

    own = g * HB
    for i in range(HB):
        xh, xl = split(GO[0, 0, i])
        r = dot(xh, VH[own + i]) + dot(xl, VH[own + i]) + dot(xh, VL[own + i])
        PA[g, i] = jnp.sum(U[own + i] * r, axis=0, keepdims=True)

    peers = (sib, far, far_sib)
    p_copies = [
        pltpu.make_async_remote_copy(
            src_ref=PA.at[g], dst_ref=PA.at[g], send_sem=p_send.at[i], recv_sem=p_recv.at[i],
            device_id=d, device_id_type=MESH,
        )
        for i, d in enumerate(peers)
    ]
    for cp in p_copies:
        cp.start()

    def back(j, i):
        uh, ul = split(U[j * HB + i] * PA[j, i])
        vh, vl = VH[j * HB + i], VL[j * HB + i]
        return dot_nt(uh, vh) + dot_nt(ul, vh) + dot_nt(uh, vl)

    def put_pair(ref, i, v):
        ref[i, 0] = v[:, :128]
        ref[i, 1] = v[:, 128:]

    for i in range(HB):
        put_pair(mom_out, i, GO[0, 0, i] - back(g, i))
    lat_out[...] = LAT[...].astype(BF16)

    for cp in sends:
        cp.wait_send()

    @pl.loop(0, 4)
    def _(k):
        for m in range(3):
            for d in range(2):
                copy_m(m, d, k, 0).wait_send()
                copy_m(m, d, k, 1).wait_send()
        y_copy(k, 0).wait_send()
        y_copy(k, 1).wait_send()

    for m in range(3):
        for d in range(2):
            t_copy(m, d, 0).wait_send()
            t_copy(m, d, 1).wait_send()
    w_store.wait()

    for cp in p_copies:
        cp.wait_recv()
    for i in range(HB):
        put_pair(upd_out, i, 0.25 * ((back(0, i) + back(1, i)) + (back(2, i) + back(3, i))))
    for cp in p_copies:
        cp.wait_send()


def finish_kernel(
    og_ref, w_ref, mom_ref, upd_ref, lat_ref,
    grad_out, mom_out, upd_out, lat_out,
    O, W, G, MI, UI, L, MO, packed, UO, w_sem, g_sem, sem,
):
    parts, cols = G.shape[0], G.shape[2]

    def copy(src, dst, s):
        cp = pltpu.make_async_copy(src, dst, s)
        cp.start()
        return cp

    o_load = copy(og_ref, O, sem.at[0])
    w_loads = [
        copy(w_ref.at[pl.ds(cols * i, cols)], W.at[pl.ds(cols * i, cols)], w_sem.at[i])
        for i in range(parts)
    ]
    l_load = copy(lat_ref, L, sem.at[1])
    m_load = copy(mom_ref, MI, sem.at[2])
    u_load = copy(upd_ref, UI, sem.at[3])
    stores = []
    o_load.wait()
    for i in range(parts):
        w_loads[i].wait()
        G[i] = dot_nt(O[...], W[cols * i : cols * i + cols, :]).astype(BF16)
        stores.append(copy(G.at[i], grad_out.at[:, pl.ds(cols * i, cols)], g_sem.at[i]))
    l_load.wait()
    stores.append(copy(L, lat_out, sem.at[4]))
    low = lane_low((32, 128))

    def pack(ref, put):
        for i in range(HB):
            for v in range(2):
                a = ref[i, v, pl.ds(0, 32, stride=2), :]
                b = ref[i, v, pl.ds(1, 32, stride=2), :]
                put(4 * i + 2 * v, jnp.where(low, a, pltpu.roll(b, 64, 1)))
                put(4 * i + 2 * v + 1, jnp.where(low, pltpu.roll(a, 64, 1), b))

    def put_mom(t, v):
        MO[t] = v

    def put_upd(t, v):
        packed[32 * t : 32 * t + 32, :] = v

    m_load.wait()
    pack(MI, put_mom)
    stores.append(copy(MO, mom_out, sem.at[5]))
    u_load.wait()
    pack(UI, put_upd)
    for m in range(32):
        UO[:, 128 * m : 128 * m + 128] = packed[pl.ds(m, 28, stride=32), :]
    stores.append(copy(UO, upd_out, sem.at[6]))
    for cp in stores:
        cp.wait()


def on_device(tokens, out_grad, proj_weight, momentum, freq_index):
    grad_scale = 1.0 / math.sqrt(TOK * 32)
    any_spec = pl.BlockSpec(memory_space=pl.ANY)
    vmem = pl.BlockSpec(memory_space=pltpu.VMEM)
    dma = pltpu.SemaphoreType.DMA
    full, mom_hb, upd_hb, lat = pl.pallas_call(
        functools.partial(kernel, grad_scale),
        out_shape=(
            jax.ShapeDtypeStruct((32, 2, 112, KV), BF16),
            jax.ShapeDtypeStruct((HB, 2, SIDE, 128), F32),
            jax.ShapeDtypeStruct((HB, 2, SIDE, 128), F32),
            jax.ShapeDtypeStruct((TOK, KV), BF16),
        ),
        in_specs=[any_spec, any_spec, any_spec, any_spec, any_spec, vmem],
        out_specs=(any_spec, vmem, vmem, vmem),
        scratch_shapes=[
            pltpu.VMEM((TOK, WIDE), BF16),
            pltpu.VMEM((WIDE, TOK), BF16),
            pltpu.VMEM((TOK, KV), BF16),
            pltpu.VMEM((32, 2, 112, KV), BF16),
            pltpu.VMEM((4, 8, 64, 256), F32),
            pltpu.VMEM((3, 2, 4, 2, HB, 32, 256), I16),
            pltpu.VMEM((3, 2, 4, 2, 128), F32),
            pltpu.VMEM((3, 2, 4, 2, HB, 32, 256), I16),
            pltpu.VMEM((3, 2, 4, 2, 128), F32),
            pltpu.VMEM((2, 4, 2, HB, 32, 256), F32),
            pltpu.VMEM((4, 2, HB, 64, 256), F32),
            pltpu.VMEM((4, 2, HB, 32, 256), I16),
            pltpu.VMEM((4, 2, 128), F32),
            pltpu.VMEM((4, 2, HB, 32, 256), I16),
            pltpu.VMEM((4, 2, 128), F32),
            pltpu.VMEM((3, 2, HB, 32, 256), I16),
            pltpu.VMEM((3, 2, 1, 128), F32),
            pltpu.VMEM((3, 2, HB, 32, 256), I16),
            pltpu.VMEM((3, 2, 1, 128), F32),
            pltpu.VMEM((4 * HB, 256, 128), BF16),
            pltpu.VMEM((4 * HB, 256, 128), BF16),
            pltpu.VMEM((4 * HB, 64, 128), F32),
            pltpu.VMEM((4, HB, 1, 128), F32),
            pltpu.VMEM((4 * HB, 32, 128), F32),
            pltpu.VMEM((HB, 2, SIDE, 128), F32),
            pltpu.VMEM((4 * HB, 4, 32), jnp.int32),
            pltpu.VMEM((TOK, KV), F32),
            dma((9,)),
            dma((4,)),
            dma((31,)),
            dma((31,)),
            dma((31,)),
            dma((31,)),
            dma((3, 2, 4, 2)),
            dma((3, 2, 4, 2)),
            dma((4, 2)),
            dma((4, 2)),
            dma((3, 2, 2)),
            dma((3, 2, 2)),
            dma((3,)),
            dma((3,)),
        ],
        compiler_params=pltpu.CompilerParams(
            collective_id=0, has_side_effects=True, vmem_limit_bytes=62 << 20
        ),
        cost_estimate=pl.CostEstimate(
            flops=8 * 10**9, bytes_accessed=24 * 10**6, transcendentals=0
        ),
    )(
        tokens,
        out_grad,
        proj_weight.reshape(2, 112, KV),
        momentum.reshape(4 * HB, 32, 128),
        freq_index.transpose(1, 0, 2),
        jnp.asarray(cosine_tables()),
    )
    parts = 8
    cols = WIDE // parts
    grad_in, mom_out, upd, latent = pl.pallas_call(
        finish_kernel,
        out_shape=(
            jax.ShapeDtypeStruct((TOK, WIDE), BF16),
            jax.ShapeDtypeStruct((4 * HB, 32, 128), F32),
            jax.ShapeDtypeStruct((4 * HB, SIDE * SIDE), F32),
            jax.ShapeDtypeStruct((TOK, KV), BF16),
        ),
        in_specs=[any_spec] * 5,
        out_specs=(any_spec,) * 4,
        scratch_shapes=[
            pltpu.VMEM((TOK, KV), BF16),
            pltpu.VMEM((WIDE, KV), BF16),
            pltpu.VMEM((parts, TOK, cols), BF16),
            pltpu.VMEM((HB, 2, SIDE, 128), F32),
            pltpu.VMEM((HB, 2, SIDE, 128), F32),
            pltpu.VMEM((TOK, KV), BF16),
            pltpu.VMEM((4 * HB, 32, 128), F32),
            pltpu.VMEM((28 * 32, 128), F32),
            pltpu.VMEM((4 * HB, SIDE * SIDE), F32),
            dma((parts,)),
            dma((parts,)),
            dma((7,)),
        ],
        compiler_params=pltpu.CompilerParams(vmem_limit_bytes=62 << 20),
        cost_estimate=pl.CostEstimate(
            flops=4 * 10**9, bytes_accessed=16 * 10**6, transcendentals=0
        ),
    )(out_grad, full.reshape(WIDE, KV), mom_hb, upd_hb, lat)
    return latent, grad_in, mom_out.reshape(1, 4 * HB, SIDE * SIDE), upd


def solution(mesh):
    return jax.shard_map(
        on_device,
        mesh=mesh,
        in_specs=(
            P(("group", "fsdp"), None),
            P(("group", "fsdp"), None),
            P("fsdp", None),
            P("group", "fsdp", None),
            P(None, "fsdp", None),
        ),
        out_specs=(
            P(("group", "fsdp"), None),
            P(("group", "fsdp"), None),
            P("group", "fsdp", None),
            P("fsdp", None),
        ),
        check_vma=False,
    )
```

```python
import functools
import math

import jax
import jax.numpy as jnp
import numpy as np
from jax import lax
from jax.experimental import pallas as pl
from jax.experimental.pallas import tpu as pltpu
from jax.sharding import PartitionSpec as P

SIDE = 64
HB = 7
DECAY = 0.9
MESH = pl.DeviceIdType.MESH
F32 = jnp.float32
BF16 = jnp.bfloat16
I16 = jnp.int16
TOK, WIDE, KV = 512, 7168, 512


def cosine_tables():
    n = np.arange(SIDE, dtype=np.float64)
    k = n[:, None]
    scale = np.where(k == 0, math.sqrt(1.0 / SIDE), math.sqrt(2.0 / SIDE))
    table = scale * np.cos(math.pi * (2.0 * n[None, :] + 1.0) * k / (2.0 * SIDE))
    t = table.T.astype(np.float32)
    high = t.astype(jnp.bfloat16)
    low = (t - high.astype(np.float32)).astype(jnp.bfloat16)
    return np.concatenate([high, low], axis=0)


def rem4(v):
    return lax.rem(v + 4, 4)


def dot(a, b):
    return jnp.dot(a, b, preferred_element_type=F32)


def dot_nt(a, b):
    return lax.dot_general(a, b, (((1,), (1,)), ((), ())), preferred_element_type=F32)


def split(v):
    high = v.astype(BF16)
    return high, (v - high.astype(F32)).astype(BF16)


def quantize(v, q_ref, s_ref, row):
    a = jnp.max(jnp.max(jnp.abs(v), axis=0), axis=0, keepdims=True)
    m = jnp.maximum(jnp.maximum(a[:, :128], a[:, 128:]), 1e-30)
    s = m * (1.0 / 32760.0)
    inv = 1.0 / s
    inv2 = jnp.concatenate([inv, inv], axis=1)[None]
    q_ref[...] = jnp.round(v * inv2).astype(jnp.int32).astype(I16)
    s_ref[pl.ds(row, 1), :] = s


def dequantize(q_ref, s_ref, row):
    s = s_ref[pl.ds(row, 1), :]
    s2 = jnp.concatenate([s, s], axis=1)[None]
    return q_ref[...].astype(jnp.int32).astype(F32) * s2


def lane_low(shape):
    return lax.broadcasted_iota(jnp.int32, shape, len(shape) - 1) < 64


def kernel(
    grad_scale,
    tok_ref, og_ref, w_ref, mom_ref, freq_ref, ct_ref,
    w_out, mom_out, upd_out, lat_out,
    T, TT, O, W, tmp, SQ, SS, RQ, RS, GH, GO, YQ, YS, ZQ, ZS, TQ, TS, VQ, VS, VH, VL, U, PA, MP, MH, FR, LAT,
    load_sem, w_sem, ag_send, ag_recv, core_send, core_recv,
    m_send, m_recv, y_send, y_recv, t_send, t_recv, p_send, p_recv,
):
    g = lax.axis_index("group")
    f = lax.axis_index("fsdp")
    c = lax.rem(g, 2)
    yh = lax.div(g, 2)
    z, yl, x = lax.div(f, 8), lax.rem(lax.div(f, 4), 2), lax.rem(f, 4)
    p0 = x * (1 - c) + z * c
    s0 = z * (1 - c) + x * c

    def f_of(p, s, y):
        xx = p * (1 - c) + s * c
        zz = s * (1 - c) + p * c
        return zz * 8 + y * 4 + xx

    def at_ps(dp, ds):
        return (g, f_of(rem4(p0 + dp), rem4(s0 + ds), yl))

    def at_y(dy):
        yy = rem4(yh * 2 + yl + dy)
        return (lax.div(yy, 2) * 2 + c, f_of(p0, s0, lax.rem(yy, 2)))

    sib = (yh * 2 + 1 - c, f)
    far = ((1 - yh) * 2 + c, f)
    far_sib = ((1 - yh) * 2 + 1 - c, f)
    pn = (at_ps(1, 0), at_ps(-1, 0))
    sn = (at_ps(0, 1), at_ps(0, -1))
    y_pair = (g, f_of(p0, s0, 1 - yl))
    y_cross = at_y(2 * yl - 1)
    p_far = at_ps(2, 0)

    barrier = pltpu.get_barrier_semaphore()
    for d in (*pn, p_far, *sn, y_pair, y_cross, sib, far, far_sib):
        pl.semaphore_signal(barrier, inc=1, device_id=d, device_id_type=MESH)

    S_OFF = (2, 1, 3, 0)

    og_load = pltpu.make_async_copy(og_ref, O, load_sem.at[8])
    og_load.start()
    w_load = pltpu.make_async_copy(w_ref, W.at[f], w_sem.at[0])
    w_load.start()
    tok_loads = []
    for i in range(4):
        for y in range(2):
            quad = rem4(z + S_OFF[i]) * 2 + y
            cols = pl.ds(pl.multiple_of(896 * quad, 128), 896)
            cp = pltpu.make_async_copy(tok_ref.at[:, cols], T.at[:, cols], load_sem.at[2 * i + y])
            cp.start()
            tok_loads.append(cp)
    mom_load = pltpu.make_async_copy(mom_ref, MP, w_sem.at[2])
    mom_load.start()
    freq_load = pltpu.make_async_copy(freq_ref, FR, w_sem.at[3])
    freq_load.start()

    sends = []

    def remote(src, dst, ss, rs, dev):
        cp = pltpu.make_async_remote_copy(
            src_ref=src, dst_ref=dst, send_sem=ss, recv_sem=rs, device_id=dev, device_id_type=MESH
        )
        cp.start()
        sends.append(cp)
        return cp

    def fb(j, t):
        return f_of(rem4(p0 + j), rem4(s0 + t), yl)

    def block(fi):
        return W.at[fi, c]

    core_copies = []

    def to_core(fi):
        i = len(core_copies)
        core_copies.append(remote(block(fi), block(fi), core_send.at[i], core_recv.at[i], sib))

    n_ag = [0]

    def ag(fi, dev):
        i = n_ag[0]
        n_ag[0] += 1
        return remote(block(fi), block(fi), ag_send.at[i], ag_recv.at[i], dev)

    def s_out(j, t):
        return ag(fb(j, t), y_pair if j == 2 else y_cross)

    a_p, a_s, a_y, a_f = [], {}, [], []

    def ag1():
        w_load.wait()
        for d in (*pn, p_far):
            a_p.append(ag(fb(0, 0), d))
        for d in range(2):
            a_s[d, 0] = ag(fb(0, 0), sn[d])
        a_y.append(s_out(0, 0))

    def ag2():
        for cp in a_p:
            cp.wait_recv()
        for j in (3, 1, 2):
            for d in range(2):
                a_s[d, j] = ag(fb(j, 0), sn[d])
        for j in (3, 1, 2):
            a_y.append(s_out(j, 0))
            to_core(fb(j, 0))

    def ag4():
        for j in (0, 3, 1, 2):
            for d in range(2):
                a_s[d, j].wait_recv()
        for j in (0, 1):
            a_f.append(ag(fb(j, 3), sn[0]))
        for j in (2, 3):
            a_f.append(ag(fb(j, 1), sn[1]))
        for t in (3, 1):
            for j in range(4):
                a_y.append(s_out(j, t))
                to_core(fb(j, t))

    def ag5():
        for cp in a_f:
            cp.wait_recv()
        for j in range(4):
            a_y.append(s_out(j, 2))
            to_core(fb(j, 2))

    def ag6(first):
        for cp in a_y[:12] if first else a_y[12:]:
            cp.wait_recv()
        for t in (0, 3, 1) if first else (2,):
            for j in range(4):
                to_core(f_of(rem4(p0 + j), rem4(s0 + t), 1 - yl))

    def ag7(low, high):
        for cp in core_copies[low:high]:
            cp.wait_recv()

    def latent_part(y, fresh):
        @pl.loop(0, 4)
        def _(i):
            cols = pl.ds(pl.multiple_of(896 * (2 * i + y), 128), 896)
            w = W[pl.ds(8 * i + 4 * y, 4)].reshape(896, KV)
            part = dot(T[:, cols], w)
            if fresh:

                @pl.when(i == 0)
                def _():
                    LAT[...] = part

                @pl.when(i > 0)
                def _():
                    LAT[...] += part
            else:
                LAT[...] += part

    def transpose(i):
        for y in range(2):
            tok_loads[2 * i + y].wait()
            quad = rem4(z + S_OFF[i]) * 2 + y

            @pl.loop(0, 7)
            def _(b):
                col = pl.multiple_of(quad * 896 + b * 128, 128)
                TT[pl.ds(col, 128), :] = T[:, pl.ds(col, 128)].T

    def chunk(dp, k, y, slot):
        fi = f_of(rem4(p0 + dp), rem4(s0 + S_OFF[k]), y)
        e = lax.rem(fi, 2)
        row = pl.multiple_of(64 * (7 * lax.div(fi, 2) + 3 * e), 64)
        res = dot(TT[pl.ds(row, 256), :], O[...])
        for i in range(4):
            for h in range(2):
                tmp[slot, 2 * i + h] = res[64 * i : 64 * i + 64, 256 * h : 256 * h + 256]
        return e

    def half(h):
        return pl.ds(32 * h, 32)

    def copy_m(m, d, k, i):
        src, dst = ((SQ, RQ), (SS, RS))[i]
        return pltpu.make_async_remote_copy(
            src_ref=src.at[m, d, k], dst_ref=dst.at[m, d, k], send_sem=m_send.at[m, d, k, i],
            recv_sem=m_recv.at[m, d, k, i], device_id=pn[d], device_id_type=MESH,
        )

    def send_m(m, d, k):
        copy_m(m, d, k, 0).start()
        copy_m(m, d, k, 1).start()

    def recv_m(m, d, k):
        copy_m(m, d, k, 0).wait_recv()
        copy_m(m, d, k, 1).wait_recv()

    def prepare(i):
        fr4 = jnp.concatenate([FR[4 * i + t] for t in range(4)], axis=1)
        for j in range(4):
            fr = fr4[j : j + 1, :]
            iota = lax.broadcasted_iota(jnp.int32, (64, 128), 0)
            eu = (iota == lax.shift_right_logical(fr, 6)).astype(F32).astype(BF16)
            ev = (iota == (fr & 63)).astype(F32).astype(BF16)
            res = dot(ct_ref[...], jnp.concatenate([eu, ev], axis=1))
            U[j * HB + i] = res[:64, :128] + res[64:, :128]
            lane = lax.broadcasted_iota(jnp.int32, (64, 128), 1)
            for t in range(4):
                mine = lax.shift_right_logical(lane, 5) == t
                rows = slice(64 * t, 64 * t + 64)
                VH[j * HB + i, rows, :] = jnp.where(mine, res[:64, 128:], 0.0).astype(BF16)
                VL[j * HB + i, rows, :] = jnp.where(mine, res[64:, 128:], 0.0).astype(BF16)

    def unpack_momentum():
        mom_load.wait()
        low = lane_low((32, 128))

        @pl.loop(0, HB)
        def _(i):
            for v in range(2):
                a, b = MP[4 * i + 2 * v], MP[4 * i + 2 * v + 1]
                MH[i, v, pl.ds(0, 32, stride=2), :] = DECAY * jnp.where(low, a, pltpu.roll(b, 64, 1))
                MH[i, v, pl.ds(1, 32, stride=2), :] = DECAY * jnp.where(low, pltpu.roll(a, 64, 1), b)

    def first(k):
        for y in range(2):
            e = chunk(2, k, y, y)
            for d in range(2):
                quantize(tmp[y, pl.ds(e, 7), half(d), :], SQ.at[0, d, k, y], SS.at[0, d, k], y)

    def second(k):
        for d in range(2):
            for y in range(2):
                slot = 2 * d + y
                e = chunk(1 if d == 0 else -1, k, y, slot)
                quantize(
                    tmp[slot, pl.ds(e, 7), half(1 - d), :], SQ.at[1, d, k, y], SS.at[1, d, k], y
                )
                GH[d, k, y] = tmp[slot, pl.ds(e, 7), half(d), :]
            send_m(1, d, k)

    def third(k):
        for d in range(2):
            recv_m(0, d, k)
            for y in range(2):
                v = GH[d, k, y] + dequantize(RQ.at[0, d, k, y], RS.at[0, d, k], y)
                quantize(v, SQ.at[2, d, k, y], SS.at[2, d, k], y)
            send_m(2, d, k)

    def own_part(k):
        for y in range(2):
            e = chunk(0, k, y, y)
            GO[k, y] = tmp[y, pl.ds(e, 7)]

    def y_copy(k, i):
        src, dst = ((YQ, ZQ), (YS, ZS))[i]
        return pltpu.make_async_remote_copy(
            src_ref=src.at[k], dst_ref=dst.at[k], send_sem=y_send.at[k, i],
            recv_sem=y_recv.at[k, i], device_id=y_pair, device_id_type=MESH,
        )

    def sum_p(k):
        for d in range(2):
            recv_m(1, d, k)
            recv_m(2, d, k)

        def total(y, d):
            return (
                GO[k, y, :, half(d), :]
                + dequantize(RQ.at[2, d, k, y], RS.at[2, d, k], y)
                + dequantize(RQ.at[1, 1 - d, k, y], RS.at[1, 1 - d, k], y)
            )

        for d in range(2):
            quantize(total(1 - yl, d), YQ.at[k, d], YS.at[k], d)
        y_copy(k, 0).start()
        y_copy(k, 1).start()
        for d in range(2):
            GO[k, 0, :, half(d), :] = total(yl, d)

    def t_copy(m, d, i):
        src, dst = ((TQ, VQ), (TS, VS))[i]
        return pltpu.make_async_remote_copy(
            src_ref=src.at[m, d], dst_ref=dst.at[m, d], send_sem=t_send.at[m, d, i],
            recv_sem=t_recv.at[m, d, i], device_id=sn[d], device_id_type=MESH,
        )

    def sum_y(k):
        y_copy(k, 0).wait_recv()
        y_copy(k, 1).wait_recv()
        return [
            GO[k, 0, :, half(d), :] + dequantize(ZQ.at[k, d], ZS.at[k], d) for d in range(2)
        ]

    def send_t(m, d, v):
        quantize(v, TQ.at[m, d], TS.at[m, d], 0)
        t_copy(m, d, 0).start()
        t_copy(m, d, 1).start()

    def recv_t(m, d):
        t_copy(m, d, 0).wait_recv()
        t_copy(m, d, 1).wait_recv()
        return dequantize(VQ.at[m, d], VS.at[m, d], 0)

    def send_first(k):
        for d in range(2):
            send_m(0, d, k)

    transpose(0)
    og_load.wait()
    first(0)
    transpose(1)
    first(1)
    pl.semaphore_wait(barrier, 10)
    ag1()
    send_first(0)
    send_first(1)
    transpose(2)
    first(2)
    send_first(2)
    transpose(3)
    first(3)
    send_first(3)
    freq_load.wait()
    second(0)
    ag2()
    third(0)
    second(1)
    third(1)
    ag4()
    second(2)
    third(2)
    own_part(0)
    sum_p(0)
    second(3)
    third(3)
    ag5()
    own_part(1)
    pl.loop(0, 3)(prepare)
    sum_p(1)
    own_part(2)
    pl.loop(3, HB)(prepare)
    a = sum_y(0)
    for d in range(2):
        send_t(0, d, a[d])
    own_part(3)
    unpack_momentum()
    sum_p(2)
    a = sum_y(1)
    send_t(1, 0, a[1])
    send_t(2, 0, a[0] + recv_t(0, 0))
    ag7(0, 15)
    latent_part(yl, True)
    sum_p(3)
    ag6(True)
    a = sum_y(2)
    send_t(1, 1, a[0])
    send_t(2, 1, a[1] + recv_t(0, 1))
    ag6(False)
    ag7(15, 31)
    w_store = pltpu.make_async_copy(W, w_out, w_sem.at[1])
    w_store.start()
    latent_part(1 - yl, False)
    a = sum_y(3)
    for d in range(2):
        v = a[d] + recv_t(2, d) + recv_t(1, 1 - d)
        for h in range(2):
            cols = slice(128 * h, 128 * h + 128)
            GO[0, 0, :, half(d), cols] = v[:, :, cols] * grad_scale + MH[:, h, half(d), :]

    own = g * HB
    for i in range(HB):
        xh, xl = split(GO[0, 0, i])
        r = dot(xh, VH[own + i]) + dot(xl, VH[own + i]) + dot(xh, VL[own + i])
        PA[g, i] = jnp.sum(U[own + i] * r, axis=0, keepdims=True)

    peers = (sib, far, far_sib)
    p_copies = [
        pltpu.make_async_remote_copy(
            src_ref=PA.at[g], dst_ref=PA.at[g], send_sem=p_send.at[i], recv_sem=p_recv.at[i],
            device_id=d, device_id_type=MESH,
        )
        for i, d in enumerate(peers)
    ]
    for cp in p_copies:
        cp.start()

    def back(j, i):
        uh, ul = split(U[j * HB + i] * PA[j, i])
        vh, vl = VH[j * HB + i], VL[j * HB + i]
        return dot_nt(uh, vh) + dot_nt(ul, vh) + dot_nt(uh, vl)

    def put_pair(ref, i, v):
        ref[i, 0] = v[:, :128]
        ref[i, 1] = v[:, 128:]

    for i in range(HB):
        put_pair(mom_out, i, GO[0, 0, i] - back(g, i))
    lat_out[...] = LAT[...].astype(BF16)

    for cp in sends:
        cp.wait_send()

    @pl.loop(0, 4)
    def _(k):
        for m in range(3):
            for d in range(2):
                copy_m(m, d, k, 0).wait_send()
                copy_m(m, d, k, 1).wait_send()
        y_copy(k, 0).wait_send()
        y_copy(k, 1).wait_send()

    for m in range(3):
        for d in range(2):
            t_copy(m, d, 0).wait_send()
            t_copy(m, d, 1).wait_send()
    w_store.wait()

    for cp in p_copies:
        cp.wait_recv()
    for i in range(HB):
        put_pair(upd_out, i, 0.25 * ((back(0, i) + back(1, i)) + (back(2, i) + back(3, i))))
    for cp in p_copies:
        cp.wait_send()


def finish_kernel(
    og_ref, w_ref, mom_ref, upd_ref, lat_ref,
    grad_out, mom_out, upd_out, lat_out,
    O, W, G, MI, UI, L, MO, packed, UO, w_sem, g_sem, sem,
):
    parts, cols = G.shape[0], G.shape[2]

    def copy(src, dst, s):
        cp = pltpu.make_async_copy(src, dst, s)
        cp.start()
        return cp

    o_load = copy(og_ref, O, sem.at[0])
    m_load = copy(mom_ref, MI, sem.at[2])
    u_load = copy(upd_ref, UI, sem.at[3])
    w_loads = [
        copy(w_ref.at[pl.ds(cols * i, cols)], W.at[pl.ds(cols * i, cols)], w_sem.at[i])
        for i in range(parts)
    ]
    l_load = copy(lat_ref, L, sem.at[1])
    low = lane_low((32, 128))

    def pack(ref, put):
        for i in range(HB):
            for v in range(2):
                a = ref[i, v, pl.ds(0, 32, stride=2), :]
                b = ref[i, v, pl.ds(1, 32, stride=2), :]
                put(4 * i + 2 * v, jnp.where(low, a, pltpu.roll(b, 64, 1)))
                put(4 * i + 2 * v + 1, jnp.where(low, pltpu.roll(a, 64, 1), b))

    def put_mom(t, v):
        MO[t] = v

    def put_upd(t, v):
        packed[32 * t : 32 * t + 32, :] = v

    stores = []
    m_load.wait()
    pack(MI, put_mom)
    stores.append(copy(MO, mom_out, sem.at[5]))
    o_load.wait()
    for i in range(parts):
        w_loads[i].wait()
        G[i] = dot_nt(O[...], W[cols * i : cols * i + cols, :]).astype(BF16)
        stores.append(copy(G.at[i], grad_out.at[:, pl.ds(cols * i, cols)], g_sem.at[i]))
        if i == 0:
            u_load.wait()
            pack(UI, put_upd)
            for m in range(32):
                UO[:, 128 * m : 128 * m + 128] = packed[pl.ds(m, 28, stride=32), :]
            stores.append(copy(UO, upd_out, sem.at[6]))
    l_load.wait()
    stores.append(copy(L, lat_out, sem.at[4]))
    for cp in stores:
        cp.wait()


def on_device(tokens, out_grad, proj_weight, momentum, freq_index):
    grad_scale = 1.0 / math.sqrt(TOK * 32)
    any_spec = pl.BlockSpec(memory_space=pl.ANY)
    vmem = pl.BlockSpec(memory_space=pltpu.VMEM)
    dma = pltpu.SemaphoreType.DMA
    full, mom_hb, upd_hb, lat = pl.pallas_call(
        functools.partial(kernel, grad_scale),
        out_shape=(
            jax.ShapeDtypeStruct((32, 2, 112, KV), BF16),
            jax.ShapeDtypeStruct((HB, 2, SIDE, 128), F32),
            jax.ShapeDtypeStruct((HB, 2, SIDE, 128), F32),
            jax.ShapeDtypeStruct((TOK, KV), BF16),
        ),
        in_specs=[any_spec, any_spec, any_spec, any_spec, any_spec, vmem],
        out_specs=(any_spec, vmem, vmem, vmem),
        scratch_shapes=[
            pltpu.VMEM((TOK, WIDE), BF16),
            pltpu.VMEM((WIDE, TOK), BF16),
            pltpu.VMEM((TOK, KV), BF16),
            pltpu.VMEM((32, 2, 112, KV), BF16),
            pltpu.VMEM((4, 8, 64, 256), F32),
            pltpu.VMEM((3, 2, 4, 2, HB, 32, 256), I16),
            pltpu.VMEM((3, 2, 4, 2, 128), F32),
            pltpu.VMEM((3, 2, 4, 2, HB, 32, 256), I16),
            pltpu.VMEM((3, 2, 4, 2, 128), F32),
            pltpu.VMEM((2, 4, 2, HB, 32, 256), F32),
            pltpu.VMEM((4, 2, HB, 64, 256), F32),
            pltpu.VMEM((4, 2, HB, 32, 256), I16),
            pltpu.VMEM((4, 2, 128), F32),
            pltpu.VMEM((4, 2, HB, 32, 256), I16),
            pltpu.VMEM((4, 2, 128), F32),
            pltpu.VMEM((3, 2, HB, 32, 256), I16),
            pltpu.VMEM((3, 2, 1, 128), F32),
            pltpu.VMEM((3, 2, HB, 32, 256), I16),
            pltpu.VMEM((3, 2, 1, 128), F32),
            pltpu.VMEM((4 * HB, 256, 128), BF16),
            pltpu.VMEM((4 * HB, 256, 128), BF16),
            pltpu.VMEM((4 * HB, 64, 128), F32),
            pltpu.VMEM((4, HB, 1, 128), F32),
            pltpu.VMEM((4 * HB, 32, 128), F32),
            pltpu.VMEM((HB, 2, SIDE, 128), F32),
            pltpu.VMEM((4 * HB, 4, 32), jnp.int32),
            pltpu.VMEM((TOK, KV), F32),
            dma((9,)),
            dma((4,)),
            dma((31,)),
            dma((31,)),
            dma((31,)),
            dma((31,)),
            dma((3, 2, 4, 2)),
            dma((3, 2, 4, 2)),
            dma((4, 2)),
            dma((4, 2)),
            dma((3, 2, 2)),
            dma((3, 2, 2)),
            dma((3,)),
            dma((3,)),
        ],
        compiler_params=pltpu.CompilerParams(
            collective_id=0, has_side_effects=True, vmem_limit_bytes=62 << 20
        ),
        cost_estimate=pl.CostEstimate(
            flops=8 * 10**9, bytes_accessed=24 * 10**6, transcendentals=0
        ),
    )(
        tokens,
        out_grad,
        proj_weight.reshape(2, 112, KV),
        momentum.reshape(4 * HB, 32, 128),
        freq_index.transpose(1, 0, 2),
        jnp.asarray(cosine_tables()),
    )
    parts = 4
    cols = WIDE // parts
    grad_in, mom_out, upd, latent = pl.pallas_call(
        finish_kernel,
        out_shape=(
            jax.ShapeDtypeStruct((TOK, WIDE), BF16),
            jax.ShapeDtypeStruct((4 * HB, 32, 128), F32),
            jax.ShapeDtypeStruct((4 * HB, SIDE * SIDE), F32),
            jax.ShapeDtypeStruct((TOK, KV), BF16),
        ),
        in_specs=[any_spec] * 5,
        out_specs=(any_spec,) * 4,
        scratch_shapes=[
            pltpu.VMEM((TOK, KV), BF16),
            pltpu.VMEM((WIDE, KV), BF16),
            pltpu.VMEM((parts, TOK, cols), BF16),
            pltpu.VMEM((HB, 2, SIDE, 128), F32),
            pltpu.VMEM((HB, 2, SIDE, 128), F32),
            pltpu.VMEM((TOK, KV), BF16),
            pltpu.VMEM((4 * HB, 32, 128), F32),
            pltpu.VMEM((28 * 32, 128), F32),
            pltpu.VMEM((4 * HB, SIDE * SIDE), F32),
            dma((parts,)),
            dma((parts,)),
            dma((7,)),
        ],
        compiler_params=pltpu.CompilerParams(vmem_limit_bytes=62 << 20),
        cost_estimate=pl.CostEstimate(
            flops=4 * 10**9, bytes_accessed=16 * 10**6, transcendentals=0
        ),
    )(out_grad, full.reshape(WIDE, KV), mom_hb, upd_hb, lat)
    return latent, grad_in, mom_out.reshape(1, 4 * HB, SIDE * SIDE), upd


def solution(mesh):
    return jax.shard_map(
        on_device,
        mesh=mesh,
        in_specs=(
            P(("group", "fsdp"), None),
            P(("group", "fsdp"), None),
            P("fsdp", None),
            P("group", "fsdp", None),
            P(None, "fsdp", None),
        ),
        out_specs=(
            P(("group", "fsdp"), None),
            P(("group", "fsdp"), None),
            P("group", "fsdp", None),
            P("fsdp", None),
        ),
        check_vma=False,
    )
```

```python
import functools
import math

import jax
import jax.numpy as jnp
import numpy as np
from jax import lax
from jax.experimental import pallas as pl
from jax.experimental.pallas import tpu as pltpu
from jax.sharding import PartitionSpec as P

SIDE = 64
HB = 7
DECAY = 0.9
MESH = pl.DeviceIdType.MESH
F32 = jnp.float32
BF16 = jnp.bfloat16
I16 = jnp.int16
TOK, WIDE, KV = 512, 7168, 512


def cosine_tables():
    n = np.arange(SIDE, dtype=np.float64)
    k = n[:, None]
    scale = np.where(k == 0, math.sqrt(1.0 / SIDE), math.sqrt(2.0 / SIDE))
    table = scale * np.cos(math.pi * (2.0 * n[None, :] + 1.0) * k / (2.0 * SIDE))
    t = table.T.astype(np.float32)
    high = t.astype(jnp.bfloat16)
    low = (t - high.astype(np.float32)).astype(jnp.bfloat16)
    return np.concatenate([high, low], axis=0)


def rem4(v):
    return lax.rem(v + 4, 4)


def dot(a, b):
    return jnp.dot(a, b, preferred_element_type=F32)


def dot_nt(a, b):
    return lax.dot_general(a, b, (((1,), (1,)), ((), ())), preferred_element_type=F32)


def split(v):
    high = v.astype(BF16)
    return high, (v - high.astype(F32)).astype(BF16)


def quantize(v, q_ref, s_ref, row):
    a = jnp.max(jnp.max(jnp.abs(v), axis=0), axis=0, keepdims=True)
    m = jnp.maximum(jnp.maximum(a[:, :128], a[:, 128:]), 1e-30)
    s = m * (1.0 / 32760.0)
    inv = 1.0 / s
    inv2 = jnp.concatenate([inv, inv], axis=1)[None]
    q_ref[...] = jnp.round(v * inv2).astype(jnp.int32).astype(I16)
    s_ref[pl.ds(row, 1), :] = s


def dequantize(q_ref, s_ref, row):
    s = s_ref[pl.ds(row, 1), :]
    s2 = jnp.concatenate([s, s], axis=1)[None]
    return q_ref[...].astype(jnp.int32).astype(F32) * s2


def lane_low(shape):
    return lax.broadcasted_iota(jnp.int32, shape, len(shape) - 1) < 64


def kernel(
    grad_scale,
    tok_ref, og_ref, w_ref, mom_ref, freq_ref, ct_ref,
    w_out, mom_out, upd_out, lat_out,
    T, TT, O, W, tmp, SQ, SS, RQ, RS, GH, GO, YQ, YS, ZQ, ZS, TQ, TS, VQ, VS, VH, VL, U, PA, MP, MH, FR, LAT,
    FQ, FS, FZ, FT,
    load_sem, w_sem, ag_send, ag_recv, core_send, core_recv,
    m_send, m_recv, y_send, y_recv, t_send, t_recv, p_send, p_recv, f_send, f_recv,
):
    g = lax.axis_index("group")
    f = lax.axis_index("fsdp")
    c = lax.rem(g, 2)
    yh = lax.div(g, 2)
    z, yl, x = lax.div(f, 8), lax.rem(lax.div(f, 4), 2), lax.rem(f, 4)
    p0 = x * (1 - c) + z * c
    s0 = z * (1 - c) + x * c

    def f_of(p, s, y):
        xx = p * (1 - c) + s * c
        zz = s * (1 - c) + p * c
        return zz * 8 + y * 4 + xx

    def at_ps(dp, ds):
        return (g, f_of(rem4(p0 + dp), rem4(s0 + ds), yl))

    def at_y(dy):
        yy = rem4(yh * 2 + yl + dy)
        return (lax.div(yy, 2) * 2 + c, f_of(p0, s0, lax.rem(yy, 2)))

    sib = (yh * 2 + 1 - c, f)
    far = ((1 - yh) * 2 + c, f)
    far_sib = ((1 - yh) * 2 + 1 - c, f)
    pn = (at_ps(1, 0), at_ps(-1, 0))
    sn = (at_ps(0, 1), at_ps(0, -1))
    y_pair = (g, f_of(p0, s0, 1 - yl))
    y_cross = at_y(2 * yl - 1)
    p_far = at_ps(2, 0)

    barrier = pltpu.get_barrier_semaphore()
    for d in (*pn, p_far, *sn, y_pair, y_cross, sib, far, far_sib):
        pl.semaphore_signal(barrier, inc=1, device_id=d, device_id_type=MESH)

    S_OFF = (2, 1, 0, 3)
    LATE = 3

    og_load = pltpu.make_async_copy(og_ref, O, load_sem.at[8])
    og_load.start()
    w_load = pltpu.make_async_copy(w_ref, W.at[f], w_sem.at[0])
    w_load.start()
    tok_loads = {}
    for i in (0, 3, 1, 2):
        for y in range(2):
            quad = rem4(z + S_OFF[i]) * 2 + y
            cols = pl.ds(pl.multiple_of(896 * quad, 128), 896)
            cp = pltpu.make_async_copy(tok_ref.at[:, cols], T.at[:, cols], load_sem.at[2 * i + y])
            cp.start()
            tok_loads[2 * i + y] = cp
    mom_load = pltpu.make_async_copy(mom_ref, MP, w_sem.at[2])
    mom_load.start()
    freq_load = pltpu.make_async_copy(freq_ref, FR, w_sem.at[3])
    freq_load.start()

    sends = []

    def remote(src, dst, ss, rs, dev):
        cp = pltpu.make_async_remote_copy(
            src_ref=src, dst_ref=dst, send_sem=ss, recv_sem=rs, device_id=dev, device_id_type=MESH
        )
        cp.start()
        sends.append(cp)
        return cp

    def fb(j, t):
        return f_of(rem4(p0 + j), rem4(s0 + t), yl)

    def block(fi):
        return W.at[fi, c]

    core_copies = []

    def to_core(fi):
        i = len(core_copies)
        core_copies.append(remote(block(fi), block(fi), core_send.at[i], core_recv.at[i], sib))

    n_ag = [0]

    def ag(fi, dev):
        i = n_ag[0]
        n_ag[0] += 1
        return remote(block(fi), block(fi), ag_send.at[i], ag_recv.at[i], dev)

    def s_out(j, t):
        return ag(fb(j, t), y_pair if j == 2 and t != 2 else y_cross)

    a_p, a_s, a_y, a_f = [], {}, [], []

    def ag1():
        w_load.wait()
        for d in (*pn, p_far):
            a_p.append(ag(fb(0, 0), d))
        for d in range(2):
            a_s[d, 0] = ag(fb(0, 0), sn[d])
        a_y.append(s_out(0, 0))

    def ag2():
        for cp in a_p:
            cp.wait_recv()
        for j in (3, 1, 2):
            for d in range(2):
                a_s[d, j] = ag(fb(j, 0), sn[d])
        for j in (3, 1, 2):
            a_y.append(s_out(j, 0))
            to_core(fb(j, 0))

    def ag4():
        for j in (0, 3, 1, 2):
            for d in range(2):
                a_s[d, j].wait_recv()
        for j in (0, 1):
            a_f.append(ag(fb(j, 3), sn[0]))
        for j in (2, 3):
            a_f.append(ag(fb(j, 1), sn[1]))
        for t in (3, 1):
            for j in range(4):
                a_y.append(s_out(j, t))
                to_core(fb(j, t))

    def ag5():
        for cp in a_f:
            cp.wait_recv()
        for j in range(4):
            a_y.append(s_out(j, 2))
            to_core(fb(j, 2))

    def ag6(first):
        for cp in a_y[:12] if first else a_y[12:]:
            cp.wait_recv()
        for t in (0, 3, 1) if first else (2,):
            for j in range(4):
                to_core(f_of(rem4(p0 + j), rem4(s0 + t), 1 - yl))

    def ag7(low, high):
        for cp in core_copies[low:high]:
            cp.wait_recv()

    def latent_part(y, fresh):
        @pl.loop(0, 4)
        def _(i):
            cols = pl.ds(pl.multiple_of(896 * (2 * i + y), 128), 896)
            w = W[pl.ds(8 * i + 4 * y, 4)].reshape(896, KV)
            part = dot(T[:, cols], w)
            if fresh:

                @pl.when(i == 0)
                def _():
                    LAT[...] = part

                @pl.when(i > 0)
                def _():
                    LAT[...] += part
            else:
                LAT[...] += part

    def transpose(i):
        for y in range(2):
            tok_loads[2 * i + y].wait()
            quad = rem4(z + S_OFF[i]) * 2 + y

            @pl.loop(0, 7)
            def _(b):
                col = pl.multiple_of(quad * 896 + b * 128, 128)
                TT[pl.ds(col, 128), :] = T[:, pl.ds(col, 128)].T

    def chunk(dp, k, y, slot):
        fi = f_of(rem4(p0 + dp), rem4(s0 + S_OFF[k]), y)
        e = lax.rem(fi, 2)
        row = pl.multiple_of(64 * (7 * lax.div(fi, 2) + 3 * e), 64)
        res = dot(TT[pl.ds(row, 256), :], O[...])
        for i in range(4):
            for h in range(2):
                tmp[slot, 2 * i + h] = res[64 * i : 64 * i + 64, 256 * h : 256 * h + 256]
        return e

    def half(h):
        return pl.ds(32 * h, 32)

    def copy_m(m, d, k, i):
        src, dst = ((SQ, RQ), (SS, RS))[i]
        at = (m, d, k, 0) if k == LATE and i == 0 else (m, d, k)
        return pltpu.make_async_remote_copy(
            src_ref=src.at[at], dst_ref=dst.at[at], send_sem=m_send.at[m, d, k, i],
            recv_sem=m_recv.at[m, d, k, i], device_id=pn[d], device_id_type=MESH,
        )

    def send_m(m, d, k):
        copy_m(m, d, k, 0).start()
        copy_m(m, d, k, 1).start()

    def recv_m(m, d, k):
        copy_m(m, d, k, 0).wait_recv()
        copy_m(m, d, k, 1).wait_recv()

    def prepare(i):
        fr4 = jnp.concatenate([FR[4 * i + t] for t in range(4)], axis=1)
        for j in range(4):
            fr = fr4[j : j + 1, :]
            iota = lax.broadcasted_iota(jnp.int32, (64, 128), 0)
            eu = (iota == lax.shift_right_logical(fr, 6)).astype(F32).astype(BF16)
            ev = (iota == (fr & 63)).astype(F32).astype(BF16)
            res = dot(ct_ref[...], jnp.concatenate([eu, ev], axis=1))
            U[j * HB + i] = res[:64, :128] + res[64:, :128]
            lane = lax.broadcasted_iota(jnp.int32, (64, 128), 1)
            for t in range(4):
                mine = lax.shift_right_logical(lane, 5) == t
                rows = slice(64 * t, 64 * t + 64)
                VH[j * HB + i, rows, :] = jnp.where(mine, res[:64, 128:], 0.0).astype(BF16)
                VL[j * HB + i, rows, :] = jnp.where(mine, res[64:, 128:], 0.0).astype(BF16)

    def unpack_momentum():
        mom_load.wait()
        low = lane_low((32, 128))

        @pl.loop(0, HB)
        def _(i):
            for v in range(2):
                a, b = MP[4 * i + 2 * v], MP[4 * i + 2 * v + 1]
                MH[i, v, pl.ds(0, 32, stride=2), :] = DECAY * jnp.where(low, a, pltpu.roll(b, 64, 1))
                MH[i, v, pl.ds(1, 32, stride=2), :] = DECAY * jnp.where(low, pltpu.roll(a, 64, 1), b)

    def first(k):
        for y in range(2):
            e = chunk(2, k, y, y)
            for d in range(2):
                quantize(tmp[y, pl.ds(e, 7), half(d), :], SQ.at[0, d, k, y], SS.at[0, d, k], y)

    def second(k):
        for d in range(2):
            for y in range(2):
                slot = 2 * d + y
                e = chunk(1 if d == 0 else -1, k, y, slot)
                quantize(
                    tmp[slot, pl.ds(e, 7), half(1 - d), :], SQ.at[1, d, k, y], SS.at[1, d, k], y
                )
                GH[d, k, y] = tmp[slot, pl.ds(e, 7), half(d), :]
            send_m(1, d, k)

    def third(k):
        for d in range(2):
            recv_m(0, d, k)
            for y in range(2):
                v = GH[d, k, y] + dequantize(RQ.at[0, d, k, y], RS.at[0, d, k], y)
                quantize(v, SQ.at[2, d, k, y], SS.at[2, d, k], y)
            send_m(2, d, k)

    def f_copy(i, j):
        src, dst = ((FQ, FZ), (FS, FT))[j]
        return pltpu.make_async_remote_copy(
            src_ref=src.at[i], dst_ref=dst.at[i], send_sem=f_send.at[i, j],
            recv_sem=f_recv.at[i, j], device_id=y_pair, device_id_type=MESH,
        )

    F_AT = {2: 0, 1: 1, -1: 2, 0: 3}

    def y_first(dp):
        i = F_AT[dp]
        e = chunk(dp, LATE, 1 - yl, i)
        for h in range(2):
            quantize(tmp[i, pl.ds(e, 7), half(h), :], FQ.at[i, h], FS.at[i], h)

    def send_f(dp):
        for j in range(2):
            f_copy(F_AT[dp], j).start()

    def late_part(dp):
        i = F_AT[dp]
        e = chunk(dp, LATE, yl, i)
        for j in range(2):
            f_copy(i, j).wait_recv()
        return [
            tmp[i, pl.ds(e, 7), half(h), :] + dequantize(FZ.at[i, h], FT.at[i], h)
            for h in range(2)
        ]

    def put_late(m, d, v):
        quantize(v, SQ.at[m, d, LATE, 0], SS.at[m, d, LATE], 0)
        SS[m, d, LATE, pl.ds(1, 1), :] = jnp.zeros((1, 128), F32)
        send_m(m, d, LATE)

    def late_first():
        v = late_part(2)
        for d in range(2):
            put_late(0, d, v[d])

    def late_second():
        for d in range(2):
            v = late_part(1 if d == 0 else -1)
            put_late(1, d, v[1 - d])
            GH[d, LATE, 0] = v[d]

    def late_third():
        for d in range(2):
            recv_m(0, d, LATE)
            v = GH[d, LATE, 0] + dequantize(RQ.at[0, d, LATE, 0], RS.at[0, d, LATE], 0)
            put_late(2, d, v)

    def late_own():
        v = late_part(0)
        for h in range(2):
            GO[LATE, 0, :, half(h), :] = v[h]

    def late_sum():
        for d in range(2):
            recv_m(1, d, LATE)
            recv_m(2, d, LATE)
        return [
            GO[LATE, 0, :, half(d), :]
            + dequantize(RQ.at[2, d, LATE, 0], RS.at[2, d, LATE], 0)
            + dequantize(RQ.at[1, 1 - d, LATE, 0], RS.at[1, 1 - d, LATE], 0)
            for d in range(2)
        ]

    def own_part(k):
        for y in range(2):
            e = chunk(0, k, y, y)
            GO[k, y] = tmp[y, pl.ds(e, 7)]

    def y_copy(k, i):
        src, dst = ((YQ, ZQ), (YS, ZS))[i]
        return pltpu.make_async_remote_copy(
            src_ref=src.at[k], dst_ref=dst.at[k], send_sem=y_send.at[k, i],
            recv_sem=y_recv.at[k, i], device_id=y_pair, device_id_type=MESH,
        )

    def sum_p(k):
        for d in range(2):
            recv_m(1, d, k)
            recv_m(2, d, k)

        def total(y, d):
            return (
                GO[k, y, :, half(d), :]
                + dequantize(RQ.at[2, d, k, y], RS.at[2, d, k], y)
                + dequantize(RQ.at[1, 1 - d, k, y], RS.at[1, 1 - d, k], y)
            )

        for d in range(2):
            quantize(total(1 - yl, d), YQ.at[k, d], YS.at[k], d)
        y_copy(k, 0).start()
        y_copy(k, 1).start()
        for d in range(2):
            GO[k, 0, :, half(d), :] = total(yl, d)

    def t_copy(m, d, i):
        src, dst = ((TQ, VQ), (TS, VS))[i]
        return pltpu.make_async_remote_copy(
            src_ref=src.at[m, d], dst_ref=dst.at[m, d], send_sem=t_send.at[m, d, i],
            recv_sem=t_recv.at[m, d, i], device_id=sn[d], device_id_type=MESH,
        )

    def sum_y(k):
        y_copy(k, 0).wait_recv()
        y_copy(k, 1).wait_recv()
        return [
            GO[k, 0, :, half(d), :] + dequantize(ZQ.at[k, d], ZS.at[k], d) for d in range(2)
        ]

    def send_t(m, d, v):
        quantize(v, TQ.at[m, d], TS.at[m, d], 0)
        t_copy(m, d, 0).start()
        t_copy(m, d, 1).start()

    def recv_t(m, d):
        t_copy(m, d, 0).wait_recv()
        t_copy(m, d, 1).wait_recv()
        return dequantize(VQ.at[m, d], VS.at[m, d], 0)

    def send_first(k):
        for d in range(2):
            send_m(0, d, k)

    transpose(0)
    og_load.wait()
    first(0)
    transpose(3)
    y_first(2)
    pl.semaphore_wait(barrier, 10)
    ag1()
    send_first(0)
    send_f(2)
    transpose(1)
    first(1)
    send_first(1)
    transpose(2)
    first(2)
    send_first(2)
    for d in (1, -1):
        y_first(d)
        send_f(d)
    freq_load.wait()
    ag2()
    second(0)
    y_first(0)
    send_f(0)
    third(0)
    late_first()
    second(1)
    third(1)
    ag4()
    second(2)
    third(2)
    own_part(0)
    sum_p(0)
    late_second()
    late_third()
    ag5()
    own_part(1)
    pl.loop(0, 3)(prepare)
    sum_p(1)
    own_part(2)
    pl.loop(3, HB)(prepare)
    a = sum_y(0)
    for d in range(2):
        send_t(0, d, a[d])
    late_own()
    unpack_momentum()
    sum_p(2)
    a = sum_y(1)
    send_t(1, 0, a[1])
    send_t(2, 0, a[0] + recv_t(0, 0))
    a = late_sum()
    send_t(1, 1, a[0])
    send_t(2, 1, a[1] + recv_t(0, 1))
    ag7(0, 15)
    latent_part(yl, True)
    ag6(True)
    ag6(False)
    a = sum_y(2)
    for d in range(2):
        v = a[d] + recv_t(2, d) + recv_t(1, 1 - d)
        for h in range(2):
            cols = slice(128 * h, 128 * h + 128)
            GO[0, 0, :, half(d), cols] = v[:, :, cols] * grad_scale + MH[:, h, half(d), :]

    own = g * HB
    for i in range(HB):
        xh, xl = split(GO[0, 0, i])
        r = dot(xh, VH[own + i]) + dot(xl, VH[own + i]) + dot(xh, VL[own + i])
        PA[g, i] = jnp.sum(U[own + i] * r, axis=0, keepdims=True)

    peers = (sib, far, far_sib)
    p_copies = [
        pltpu.make_async_remote_copy(
            src_ref=PA.at[g], dst_ref=PA.at[g], send_sem=p_send.at[i], recv_sem=p_recv.at[i],
            device_id=d, device_id_type=MESH,
        )
        for i, d in enumerate(peers)
    ]
    for cp in p_copies:
        cp.start()

    def back(j, i):
        uh, ul = split(U[j * HB + i] * PA[j, i])
        vh, vl = VH[j * HB + i], VL[j * HB + i]
        return dot_nt(uh, vh) + dot_nt(ul, vh) + dot_nt(uh, vl)

    def put_pair(ref, i, v):
        ref[i, 0] = v[:, :128]
        ref[i, 1] = v[:, 128:]

    for i in range(HB):
        put_pair(mom_out, i, GO[0, 0, i] - back(g, i))
    ag7(15, 31)
    w_store = pltpu.make_async_copy(W, w_out, w_sem.at[1])
    w_store.start()
    latent_part(1 - yl, False)
    lat_out[...] = LAT[...].astype(BF16)

    for cp in sends:
        cp.wait_send()

    for k in range(4):
        for m in range(3):
            for d in range(2):
                copy_m(m, d, k, 0).wait_send()
                copy_m(m, d, k, 1).wait_send()
        if k != LATE:
            y_copy(k, 0).wait_send()
            y_copy(k, 1).wait_send()
        f_copy(k, 0).wait_send()
        f_copy(k, 1).wait_send()

    for m in range(3):
        for d in range(2):
            t_copy(m, d, 0).wait_send()
            t_copy(m, d, 1).wait_send()
    w_store.wait()

    for cp in p_copies:
        cp.wait_recv()
    for i in range(HB):
        put_pair(upd_out, i, 0.25 * ((back(0, i) + back(1, i)) + (back(2, i) + back(3, i))))
    for cp in p_copies:
        cp.wait_send()


def finish_kernel(
    og_ref, w_ref, mom_ref, upd_ref, lat_ref,
    grad_out, mom_out, upd_out, lat_out,
    O, W, G, MI, UI, L, MO, packed, UO, w_sem, g_sem, sem,
):
    parts, cols = G.shape[0], G.shape[2]

    def copy(src, dst, s):
        cp = pltpu.make_async_copy(src, dst, s)
        cp.start()
        return cp

    o_load = copy(og_ref, O, sem.at[0])
    m_load = copy(mom_ref, MI, sem.at[2])
    u_load = copy(upd_ref, UI, sem.at[3])
    w_loads = [
        copy(w_ref.at[pl.ds(cols * i, cols)], W.at[pl.ds(cols * i, cols)], w_sem.at[i])
        for i in range(parts)
    ]
    l_load = copy(lat_ref, L, sem.at[1])
    low = lane_low((32, 128))

    def pack(ref, put):
        for i in range(HB):
            for v in range(2):
                a = ref[i, v, pl.ds(0, 32, stride=2), :]
                b = ref[i, v, pl.ds(1, 32, stride=2), :]
                put(4 * i + 2 * v, jnp.where(low, a, pltpu.roll(b, 64, 1)))
                put(4 * i + 2 * v + 1, jnp.where(low, pltpu.roll(a, 64, 1), b))

    def put_mom(t, v):
        MO[t] = v

    def put_upd(t, v):
        packed[32 * t : 32 * t + 32, :] = v

    stores = []
    m_load.wait()
    pack(MI, put_mom)
    stores.append(copy(MO, mom_out, sem.at[5]))
    o_load.wait()
    for i in range(parts):
        w_loads[i].wait()
        G[i] = dot_nt(O[...], W[cols * i : cols * i + cols, :]).astype(BF16)
        stores.append(copy(G.at[i], grad_out.at[:, pl.ds(cols * i, cols)], g_sem.at[i]))
        if i == 0:
            u_load.wait()
            pack(UI, put_upd)
            for m in range(32):
                UO[:, 128 * m : 128 * m + 128] = packed[pl.ds(m, 28, stride=32), :]
            stores.append(copy(UO, upd_out, sem.at[6]))
    l_load.wait()
    stores.append(copy(L, lat_out, sem.at[4]))
    for cp in stores:
        cp.wait()


def on_device(tokens, out_grad, proj_weight, momentum, freq_index):
    grad_scale = 1.0 / math.sqrt(TOK * 32)
    any_spec = pl.BlockSpec(memory_space=pl.ANY)
    vmem = pl.BlockSpec(memory_space=pltpu.VMEM)
    dma = pltpu.SemaphoreType.DMA
    full, mom_hb, upd_hb, lat = pl.pallas_call(
        functools.partial(kernel, grad_scale),
        out_shape=(
            jax.ShapeDtypeStruct((32, 2, 112, KV), BF16),
            jax.ShapeDtypeStruct((HB, 2, SIDE, 128), F32),
            jax.ShapeDtypeStruct((HB, 2, SIDE, 128), F32),
            jax.ShapeDtypeStruct((TOK, KV), BF16),
        ),
        in_specs=[any_spec, any_spec, any_spec, any_spec, any_spec, vmem],
        out_specs=(any_spec, vmem, vmem, vmem),
        scratch_shapes=[
            pltpu.VMEM((TOK, WIDE), BF16),
            pltpu.VMEM((WIDE, TOK), BF16),
            pltpu.VMEM((TOK, KV), BF16),
            pltpu.VMEM((32, 2, 112, KV), BF16),
            pltpu.VMEM((4, 8, 64, 256), F32),
            pltpu.VMEM((3, 2, 4, 2, HB, 32, 256), I16),
            pltpu.VMEM((3, 2, 4, 2, 128), F32),
            pltpu.VMEM((3, 2, 4, 2, HB, 32, 256), I16),
            pltpu.VMEM((3, 2, 4, 2, 128), F32),
            pltpu.VMEM((2, 4, 2, HB, 32, 256), F32),
            pltpu.VMEM((4, 2, HB, 64, 256), F32),
            pltpu.VMEM((4, 2, HB, 32, 256), I16),
            pltpu.VMEM((4, 2, 128), F32),
            pltpu.VMEM((4, 2, HB, 32, 256), I16),
            pltpu.VMEM((4, 2, 128), F32),
            pltpu.VMEM((3, 2, HB, 32, 256), I16),
            pltpu.VMEM((3, 2, 1, 128), F32),
            pltpu.VMEM((3, 2, HB, 32, 256), I16),
            pltpu.VMEM((3, 2, 1, 128), F32),
            pltpu.VMEM((4 * HB, 256, 128), BF16),
            pltpu.VMEM((4 * HB, 256, 128), BF16),
            pltpu.VMEM((4 * HB, 64, 128), F32),
            pltpu.VMEM((4, HB, 1, 128), F32),
            pltpu.VMEM((4 * HB, 32, 128), F32),
            pltpu.VMEM((HB, 2, SIDE, 128), F32),
            pltpu.VMEM((4 * HB, 4, 32), jnp.int32),
            pltpu.VMEM((TOK, KV), F32),
            pltpu.VMEM((4, 2, HB, 32, 256), I16),
            pltpu.VMEM((4, 2, 128), F32),
            pltpu.VMEM((4, 2, HB, 32, 256), I16),
            pltpu.VMEM((4, 2, 128), F32),
            dma((9,)),
            dma((4,)),
            dma((31,)),
            dma((31,)),
            dma((31,)),
            dma((31,)),
            dma((3, 2, 4, 2)),
            dma((3, 2, 4, 2)),
            dma((4, 2)),
            dma((4, 2)),
            dma((3, 2, 2)),
            dma((3, 2, 2)),
            dma((3,)),
            dma((3,)),
            dma((4, 2)),
            dma((4, 2)),
        ],
        compiler_params=pltpu.CompilerParams(
            collective_id=0, has_side_effects=True, vmem_limit_bytes=62 << 20
        ),
        cost_estimate=pl.CostEstimate(
            flops=8 * 10**9, bytes_accessed=24 * 10**6, transcendentals=0
        ),
    )(
        tokens,
        out_grad,
        proj_weight.reshape(2, 112, KV),
        momentum.reshape(4 * HB, 32, 128),
        freq_index.transpose(1, 0, 2),
        jnp.asarray(cosine_tables()),
    )
    parts = 4
    cols = WIDE // parts
    grad_in, mom_out, upd, latent = pl.pallas_call(
        finish_kernel,
        out_shape=(
            jax.ShapeDtypeStruct((TOK, WIDE), BF16),
            jax.ShapeDtypeStruct((4 * HB, 32, 128), F32),
            jax.ShapeDtypeStruct((4 * HB, SIDE * SIDE), F32),
            jax.ShapeDtypeStruct((TOK, KV), BF16),
        ),
        in_specs=[any_spec] * 5,
        out_specs=(any_spec,) * 4,
        scratch_shapes=[
            pltpu.VMEM((TOK, KV), BF16),
            pltpu.VMEM((WIDE, KV), BF16),
            pltpu.VMEM((parts, TOK, cols), BF16),
            pltpu.VMEM((HB, 2, SIDE, 128), F32),
            pltpu.VMEM((HB, 2, SIDE, 128), F32),
            pltpu.VMEM((TOK, KV), BF16),
            pltpu.VMEM((4 * HB, 32, 128), F32),
            pltpu.VMEM((28 * 32, 128), F32),
            pltpu.VMEM((4 * HB, SIDE * SIDE), F32),
            dma((parts,)),
            dma((parts,)),
            dma((7,)),
        ],
        compiler_params=pltpu.CompilerParams(vmem_limit_bytes=62 << 20),
        cost_estimate=pl.CostEstimate(
            flops=4 * 10**9, bytes_accessed=16 * 10**6, transcendentals=0
        ),
    )(out_grad, full.reshape(WIDE, KV), mom_hb, upd_hb, lat)
    return latent, grad_in, mom_out.reshape(1, 4 * HB, SIDE * SIDE), upd


def solution(mesh):
    return jax.shard_map(
        on_device,
        mesh=mesh,
        in_specs=(
            P(("group", "fsdp"), None),
            P(("group", "fsdp"), None),
            P("fsdp", None),
            P("group", "fsdp", None),
            P(None, "fsdp", None),
        ),
        out_specs=(
            P(("group", "fsdp"), None),
            P(("group", "fsdp"), None),
            P("group", "fsdp", None),
            P("fsdp", None),
        ),
        check_vma=False,
    )
```

```python
import functools
import math

import jax
import jax.numpy as jnp
import numpy as np
from jax import lax
from jax.experimental import pallas as pl
from jax.experimental.pallas import tpu as pltpu
from jax.sharding import PartitionSpec as P

SIDE = 64
HB = 7
DECAY = 0.9
MESH = pl.DeviceIdType.MESH
F32 = jnp.float32
BF16 = jnp.bfloat16
I16 = jnp.int16
TOK, WIDE, KV = 512, 7168, 512


def cosine_tables():
    n = np.arange(SIDE, dtype=np.float64)
    k = n[:, None]
    scale = np.where(k == 0, math.sqrt(1.0 / SIDE), math.sqrt(2.0 / SIDE))
    table = scale * np.cos(math.pi * (2.0 * n[None, :] + 1.0) * k / (2.0 * SIDE))
    t = table.T.astype(np.float32)
    high = t.astype(jnp.bfloat16)
    low = (t - high.astype(np.float32)).astype(jnp.bfloat16)
    return np.concatenate([high, low], axis=0)


def rem4(v):
    return lax.rem(v + 4, 4)


def dot(a, b):
    return jnp.dot(a, b, preferred_element_type=F32)


def dot_nt(a, b):
    return lax.dot_general(a, b, (((1,), (1,)), ((), ())), preferred_element_type=F32)


def split(v):
    high = v.astype(BF16)
    return high, (v - high.astype(F32)).astype(BF16)


def quantize(v, q_ref, s_ref, row):
    a = jnp.max(jnp.max(jnp.abs(v), axis=0), axis=0, keepdims=True)
    m = jnp.maximum(jnp.maximum(a[:, :128], a[:, 128:]), 1e-30)
    s = m * (1.0 / 32760.0)
    inv = 1.0 / s
    inv2 = jnp.concatenate([inv, inv], axis=1)[None]
    q_ref[...] = jnp.round(v * inv2).astype(jnp.int32).astype(I16)
    s_ref[pl.ds(row, 1), :] = s


def dequantize(q_ref, s_ref, row):
    s = s_ref[pl.ds(row, 1), :]
    s2 = jnp.concatenate([s, s], axis=1)[None]
    return q_ref[...].astype(jnp.int32).astype(F32) * s2


def lane_low(shape):
    return lax.broadcasted_iota(jnp.int32, shape, len(shape) - 1) < 64


def kernel(
    grad_scale,
    tok_ref, og_ref, w_ref, mom_ref, freq_ref, ct_ref,
    w_out, mom_out, upd_out, lat_out,
    T, TT, O, W, tmp, SQ, SS, RQ, RS, GH, GO, YQ, YS, ZQ, ZS, TQ, TS, VQ, VS, VH, VL, U, PA, MP, MH, FR, LAT,
    FQ, FS, FZ, FT,
    load_sem, w_sem, ag_send, ag_recv, core_send, core_recv,
    m_send, m_recv, y_send, y_recv, t_send, t_recv, p_send, p_recv, f_send, f_recv, ws_sem,
):
    g = lax.axis_index("group")
    f = lax.axis_index("fsdp")
    c = lax.rem(g, 2)
    yh = lax.div(g, 2)
    z, yl, x = lax.div(f, 8), lax.rem(lax.div(f, 4), 2), lax.rem(f, 4)
    p0 = x * (1 - c) + z * c
    s0 = z * (1 - c) + x * c

    def f_of(p, s, y):
        xx = p * (1 - c) + s * c
        zz = s * (1 - c) + p * c
        return zz * 8 + y * 4 + xx

    def at_ps(dp, ds):
        return (g, f_of(rem4(p0 + dp), rem4(s0 + ds), yl))

    def at_y(dy):
        yy = rem4(yh * 2 + yl + dy)
        return (lax.div(yy, 2) * 2 + c, f_of(p0, s0, lax.rem(yy, 2)))

    sib = (yh * 2 + 1 - c, f)
    far = ((1 - yh) * 2 + c, f)
    far_sib = ((1 - yh) * 2 + 1 - c, f)
    pn = (at_ps(1, 0), at_ps(-1, 0))
    sn = (at_ps(0, 1), at_ps(0, -1))
    y_pair = (g, f_of(p0, s0, 1 - yl))
    y_cross = at_y(2 * yl - 1)
    p_far = at_ps(2, 0)

    barrier = pltpu.get_barrier_semaphore()
    for d in (*pn, p_far, *sn, y_pair, y_cross, sib, far, far_sib):
        pl.semaphore_signal(barrier, inc=1, device_id=d, device_id_type=MESH)

    S_OFF = (2, 1, 0, 3)
    LATE = 3

    og_load = pltpu.make_async_copy(og_ref, O, load_sem.at[8])
    og_load.start()
    w_load = pltpu.make_async_copy(w_ref, W.at[f], w_sem.at[0])
    w_load.start()
    tok_loads = {}
    for i in (0, 3, 1, 2):
        for y in range(2):
            quad = rem4(z + S_OFF[i]) * 2 + y
            cols = pl.ds(pl.multiple_of(896 * quad, 128), 896)
            cp = pltpu.make_async_copy(tok_ref.at[:, cols], T.at[:, cols], load_sem.at[2 * i + y])
            cp.start()
            tok_loads[2 * i + y] = cp
    mom_load = pltpu.make_async_copy(mom_ref, MP, w_sem.at[2])
    mom_load.start()
    freq_load = pltpu.make_async_copy(freq_ref, FR, w_sem.at[3])
    freq_load.start()

    sends = []

    def remote(src, dst, ss, rs, dev):
        cp = pltpu.make_async_remote_copy(
            src_ref=src, dst_ref=dst, send_sem=ss, recv_sem=rs, device_id=dev, device_id_type=MESH
        )
        cp.start()
        sends.append(cp)
        return cp

    def fb(j, t):
        return f_of(rem4(p0 + j), rem4(s0 + t), yl)

    def block(fi):
        return W.at[fi, c]

    core_copies = []

    def to_core(fi):
        i = len(core_copies)
        core_copies.append(remote(block(fi), block(fi), core_send.at[i], core_recv.at[i], sib))

    n_ag = [0]

    def ag(fi, dev):
        i = n_ag[0]
        n_ag[0] += 1
        return remote(block(fi), block(fi), ag_send.at[i], ag_recv.at[i], dev)

    def s_out(j, t):
        return ag(fb(j, t), y_pair if j == 2 and t != 2 else y_cross)

    a_p, a_s, a_y, a_f = [], {}, [], []

    def ag1():
        w_load.wait()
        for d in (*pn, p_far):
            a_p.append(ag(fb(0, 0), d))
        for d in range(2):
            a_s[d, 0] = ag(fb(0, 0), sn[d])
        a_y.append(s_out(0, 0))

    def ag2():
        for cp in a_p:
            cp.wait_recv()
        for j in (3, 1, 2):
            for d in range(2):
                a_s[d, j] = ag(fb(j, 0), sn[d])
        for j in (3, 1, 2):
            a_y.append(s_out(j, 0))
            to_core(fb(j, 0))

    def ag4():
        for j in (0, 3, 1, 2):
            for d in range(2):
                a_s[d, j].wait_recv()
        for j in (0, 1):
            a_f.append(ag(fb(j, 3), sn[0]))
        for j in (2, 3):
            a_f.append(ag(fb(j, 1), sn[1]))
        for t in (3, 1):
            for j in range(4):
                a_y.append(s_out(j, t))
                to_core(fb(j, t))

    def ag5():
        for cp in a_f:
            cp.wait_recv()
        for j in range(4):
            a_y.append(s_out(j, 2))
            to_core(fb(j, 2))

    def ag6(first):
        for cp in a_y[:12] if first else a_y[12:]:
            cp.wait_recv()
        for t in (0, 3, 1) if first else (2,):
            for j in range(4):
                to_core(f_of(rem4(p0 + j), rem4(s0 + t), 1 - yl))

    def ag7(low, high):
        for cp in core_copies[low:high]:
            cp.wait_recv()

    def store_plane(y, base):
        copies = []
        for i in range(4):
            rows = pl.ds(8 * i + 4 * y, 4)
            cp = pltpu.make_async_copy(W.at[rows], w_out.at[rows], ws_sem.at[base + i])
            cp.start()
            copies.append(cp)
        return copies

    def latent_part(y, fresh):
        @pl.loop(0, 4)
        def _(i):
            cols = pl.ds(pl.multiple_of(896 * (2 * i + y), 128), 896)
            w = W[pl.ds(8 * i + 4 * y, 4)].reshape(896, KV)
            part = dot(T[:, cols], w)
            if fresh:

                @pl.when(i == 0)
                def _():
                    LAT[...] = part

                @pl.when(i > 0)
                def _():
                    LAT[...] += part
            else:
                LAT[...] += part

    def transpose(i):
        for y in range(2):
            tok_loads[2 * i + y].wait()
            quad = rem4(z + S_OFF[i]) * 2 + y

            @pl.loop(0, 7)
            def _(b):
                col = pl.multiple_of(quad * 896 + b * 128, 128)
                TT[pl.ds(col, 128), :] = T[:, pl.ds(col, 128)].T

    def chunk(dp, k, y, slot):
        fi = f_of(rem4(p0 + dp), rem4(s0 + S_OFF[k]), y)
        e = lax.rem(fi, 2)
        row = pl.multiple_of(64 * (7 * lax.div(fi, 2) + 3 * e), 64)
        res = dot(TT[pl.ds(row, 256), :], O[...])
        for i in range(4):
            for h in range(2):
                tmp[slot, 2 * i + h] = res[64 * i : 64 * i + 64, 256 * h : 256 * h + 256]
        return e

    def half(h):
        return pl.ds(32 * h, 32)

    def copy_m(m, d, k, i):
        src, dst = ((SQ, RQ), (SS, RS))[i]
        at = (m, d, k, 0) if k == LATE and i == 0 else (m, d, k)
        return pltpu.make_async_remote_copy(
            src_ref=src.at[at], dst_ref=dst.at[at], send_sem=m_send.at[m, d, k, i],
            recv_sem=m_recv.at[m, d, k, i], device_id=pn[d], device_id_type=MESH,
        )

    def send_m(m, d, k):
        copy_m(m, d, k, 0).start()
        copy_m(m, d, k, 1).start()

    def recv_m(m, d, k):
        copy_m(m, d, k, 0).wait_recv()
        copy_m(m, d, k, 1).wait_recv()

    def prepare(i):
        fr4 = jnp.concatenate([FR[4 * i + t] for t in range(4)], axis=1)
        for j in range(4):
            fr = fr4[j : j + 1, :]
            iota = lax.broadcasted_iota(jnp.int32, (64, 128), 0)
            eu = (iota == lax.shift_right_logical(fr, 6)).astype(F32).astype(BF16)
            ev = (iota == (fr & 63)).astype(F32).astype(BF16)
            res = dot(ct_ref[...], jnp.concatenate([eu, ev], axis=1))
            U[j * HB + i] = res[:64, :128] + res[64:, :128]
            lane = lax.broadcasted_iota(jnp.int32, (64, 128), 1)
            for t in range(4):
                mine = lax.shift_right_logical(lane, 5) == t
                rows = slice(64 * t, 64 * t + 64)
                VH[j * HB + i, rows, :] = jnp.where(mine, res[:64, 128:], 0.0).astype(BF16)
                VL[j * HB + i, rows, :] = jnp.where(mine, res[64:, 128:], 0.0).astype(BF16)

    def unpack_momentum():
        mom_load.wait()
        low = lane_low((32, 128))

        @pl.loop(0, HB)
        def _(i):
            for v in range(2):
                a, b = MP[4 * i + 2 * v], MP[4 * i + 2 * v + 1]
                MH[i, v, pl.ds(0, 32, stride=2), :] = DECAY * jnp.where(low, a, pltpu.roll(b, 64, 1))
                MH[i, v, pl.ds(1, 32, stride=2), :] = DECAY * jnp.where(low, pltpu.roll(a, 64, 1), b)

    def first(k):
        for y in range(2):
            e = chunk(2, k, y, y)
            for d in range(2):
                quantize(tmp[y, pl.ds(e, 7), half(d), :], SQ.at[0, d, k, y], SS.at[0, d, k], y)

    def second(k):
        for d in range(2):
            for y in range(2):
                slot = 2 * d + y
                e = chunk(1 if d == 0 else -1, k, y, slot)
                quantize(
                    tmp[slot, pl.ds(e, 7), half(1 - d), :], SQ.at[1, d, k, y], SS.at[1, d, k], y
                )
                GH[d, k, y] = tmp[slot, pl.ds(e, 7), half(d), :]
            send_m(1, d, k)

    def third(k):
        for d in range(2):
            recv_m(0, d, k)
            for y in range(2):
                v = GH[d, k, y] + dequantize(RQ.at[0, d, k, y], RS.at[0, d, k], y)
                quantize(v, SQ.at[2, d, k, y], SS.at[2, d, k], y)
            send_m(2, d, k)

    def f_copy(i, j):
        src, dst = ((FQ, FZ), (FS, FT))[j]
        return pltpu.make_async_remote_copy(
            src_ref=src.at[i], dst_ref=dst.at[i], send_sem=f_send.at[i, j],
            recv_sem=f_recv.at[i, j], device_id=y_pair, device_id_type=MESH,
        )

    F_AT = {2: 0, 1: 1, -1: 2, 0: 3}

    def y_first(dp):
        i = F_AT[dp]
        e = chunk(dp, LATE, 1 - yl, i)
        for h in range(2):
            quantize(tmp[i, pl.ds(e, 7), half(h), :], FQ.at[i, h], FS.at[i], h)

    def send_f(dp):
        for j in range(2):
            f_copy(F_AT[dp], j).start()

    def late_part(dp):
        i = F_AT[dp]
        e = chunk(dp, LATE, yl, i)
        for j in range(2):
            f_copy(i, j).wait_recv()
        return [
            tmp[i, pl.ds(e, 7), half(h), :] + dequantize(FZ.at[i, h], FT.at[i], h)
            for h in range(2)
        ]

    def put_late(m, d, v):
        quantize(v, SQ.at[m, d, LATE, 0], SS.at[m, d, LATE], 0)
        SS[m, d, LATE, pl.ds(1, 1), :] = jnp.zeros((1, 128), F32)
        send_m(m, d, LATE)

    def late_first():
        v = late_part(2)
        for d in range(2):
            put_late(0, d, v[d])

    def late_second():
        for d in range(2):
            v = late_part(1 if d == 0 else -1)
            put_late(1, d, v[1 - d])
            GH[d, LATE, 0] = v[d]

    def late_third():
        for d in range(2):
            recv_m(0, d, LATE)
            v = GH[d, LATE, 0] + dequantize(RQ.at[0, d, LATE, 0], RS.at[0, d, LATE], 0)
            put_late(2, d, v)

    def late_own():
        v = late_part(0)
        for h in range(2):
            GO[LATE, 0, :, half(h), :] = v[h]

    def late_sum():
        for d in range(2):
            recv_m(1, d, LATE)
            recv_m(2, d, LATE)
        return [
            GO[LATE, 0, :, half(d), :]
            + dequantize(RQ.at[2, d, LATE, 0], RS.at[2, d, LATE], 0)
            + dequantize(RQ.at[1, 1 - d, LATE, 0], RS.at[1, 1 - d, LATE], 0)
            for d in range(2)
        ]

    def own_part(k):
        for y in range(2):
            e = chunk(0, k, y, y)
            GO[k, y] = tmp[y, pl.ds(e, 7)]

    def y_copy(k, i):
        src, dst = ((YQ, ZQ), (YS, ZS))[i]
        return pltpu.make_async_remote_copy(
            src_ref=src.at[k], dst_ref=dst.at[k], send_sem=y_send.at[k, i],
            recv_sem=y_recv.at[k, i], device_id=y_pair, device_id_type=MESH,
        )

    def sum_p(k):
        for d in range(2):
            recv_m(1, d, k)
            recv_m(2, d, k)

        def total(y, d):
            return (
                GO[k, y, :, half(d), :]
                + dequantize(RQ.at[2, d, k, y], RS.at[2, d, k], y)
                + dequantize(RQ.at[1, 1 - d, k, y], RS.at[1, 1 - d, k], y)
            )

        for d in range(2):
            quantize(total(1 - yl, d), YQ.at[k, d], YS.at[k], d)
        y_copy(k, 0).start()
        y_copy(k, 1).start()
        for d in range(2):
            GO[k, 0, :, half(d), :] = total(yl, d)

    def t_copy(m, d, i):
        src, dst = ((TQ, VQ), (TS, VS))[i]
        return pltpu.make_async_remote_copy(
            src_ref=src.at[m, d], dst_ref=dst.at[m, d], send_sem=t_send.at[m, d, i],
            recv_sem=t_recv.at[m, d, i], device_id=sn[d], device_id_type=MESH,
        )

    def sum_y(k):
        y_copy(k, 0).wait_recv()
        y_copy(k, 1).wait_recv()
        return [
            GO[k, 0, :, half(d), :] + dequantize(ZQ.at[k, d], ZS.at[k], d) for d in range(2)
        ]

    def send_t(m, d, v):
        quantize(v, TQ.at[m, d], TS.at[m, d], 0)
        t_copy(m, d, 0).start()
        t_copy(m, d, 1).start()

    def recv_t(m, d):
        t_copy(m, d, 0).wait_recv()
        t_copy(m, d, 1).wait_recv()
        return dequantize(VQ.at[m, d], VS.at[m, d], 0)

    def send_first(k):
        for d in range(2):
            send_m(0, d, k)

    transpose(0)
    og_load.wait()
    first(0)
    transpose(3)
    y_first(2)
    pl.semaphore_wait(barrier, 10)
    ag1()
    send_first(0)
    send_f(2)
    transpose(1)
    first(1)
    send_first(1)
    transpose(2)
    first(2)
    send_first(2)
    for d in (1, -1):
        y_first(d)
        send_f(d)
    freq_load.wait()
    ag2()
    second(0)
    y_first(0)
    send_f(0)
    third(0)
    late_first()
    second(1)
    third(1)
    ag4()
    second(2)
    third(2)
    own_part(0)
    sum_p(0)
    late_second()
    late_third()
    ag5()
    own_part(1)
    pl.loop(0, 3)(prepare)
    sum_p(1)
    own_part(2)
    pl.loop(3, HB)(prepare)
    a = sum_y(0)
    for d in range(2):
        send_t(0, d, a[d])
    late_own()
    unpack_momentum()
    sum_p(2)
    a = sum_y(1)
    send_t(1, 0, a[1])
    send_t(2, 0, a[0] + recv_t(0, 0))
    a = late_sum()
    send_t(1, 1, a[0])
    send_t(2, 1, a[1] + recv_t(0, 1))
    ag7(0, 15)
    w_stores = store_plane(yl, 0)
    latent_part(yl, True)
    ag6(True)
    ag6(False)
    a = sum_y(2)
    for d in range(2):
        v = a[d] + recv_t(2, d) + recv_t(1, 1 - d)
        for h in range(2):
            cols = slice(128 * h, 128 * h + 128)
            GO[0, 0, :, half(d), cols] = v[:, :, cols] * grad_scale + MH[:, h, half(d), :]

    own = g * HB
    for i in range(HB):
        xh, xl = split(GO[0, 0, i])
        r = dot(xh, VH[own + i]) + dot(xl, VH[own + i]) + dot(xh, VL[own + i])
        PA[g, i] = jnp.sum(U[own + i] * r, axis=0, keepdims=True)

    peers = (sib, far, far_sib)
    p_copies = [
        pltpu.make_async_remote_copy(
            src_ref=PA.at[g], dst_ref=PA.at[g], send_sem=p_send.at[i], recv_sem=p_recv.at[i],
            device_id=d, device_id_type=MESH,
        )
        for i, d in enumerate(peers)
    ]
    for cp in p_copies:
        cp.start()

    def back(j, i):
        uh, ul = split(U[j * HB + i] * PA[j, i])
        vh, vl = VH[j * HB + i], VL[j * HB + i]
        return dot_nt(uh, vh) + dot_nt(ul, vh) + dot_nt(uh, vl)

    def put_pair(ref, i, v):
        ref[i, 0] = v[:, :128]
        ref[i, 1] = v[:, 128:]

    for i in range(HB):
        put_pair(mom_out, i, GO[0, 0, i] - back(g, i))
    ag7(15, 31)
    w_stores += store_plane(1 - yl, 4)
    latent_part(1 - yl, False)
    lat_out[...] = LAT[...].astype(BF16)

    for cp in sends:
        cp.wait_send()

    for k in range(4):
        for m in range(3):
            for d in range(2):
                copy_m(m, d, k, 0).wait_send()
                copy_m(m, d, k, 1).wait_send()
        if k != LATE:
            y_copy(k, 0).wait_send()
            y_copy(k, 1).wait_send()
        f_copy(k, 0).wait_send()
        f_copy(k, 1).wait_send()

    for m in range(3):
        for d in range(2):
            t_copy(m, d, 0).wait_send()
            t_copy(m, d, 1).wait_send()
    for cp in w_stores:
        cp.wait()

    for cp in p_copies:
        cp.wait_recv()
    for i in range(HB):
        put_pair(upd_out, i, 0.25 * ((back(0, i) + back(1, i)) + (back(2, i) + back(3, i))))
    for cp in p_copies:
        cp.wait_send()


def finish_kernel(
    og_ref, w_ref, mom_ref, upd_ref, lat_ref,
    grad_out, mom_out, upd_out, lat_out,
    O, W, G, MI, UI, L, MO, packed, UO, w_sem, g_sem, sem,
):
    parts, cols = G.shape[0], G.shape[2]

    def copy(src, dst, s):
        cp = pltpu.make_async_copy(src, dst, s)
        cp.start()
        return cp

    o_load = copy(og_ref, O, sem.at[0])
    m_load = copy(mom_ref, MI, sem.at[2])
    u_load = copy(upd_ref, UI, sem.at[3])
    w_loads = [
        copy(w_ref.at[pl.ds(cols * i, cols)], W.at[pl.ds(cols * i, cols)], w_sem.at[i])
        for i in range(parts)
    ]
    l_load = copy(lat_ref, L, sem.at[1])
    low = lane_low((32, 128))

    def pack(ref, put):
        for i in range(HB):
            for v in range(2):
                a = ref[i, v, pl.ds(0, 32, stride=2), :]
                b = ref[i, v, pl.ds(1, 32, stride=2), :]
                put(4 * i + 2 * v, jnp.where(low, a, pltpu.roll(b, 64, 1)))
                put(4 * i + 2 * v + 1, jnp.where(low, pltpu.roll(a, 64, 1), b))

    def put_mom(t, v):
        MO[t] = v

    def put_upd(t, v):
        packed[32 * t : 32 * t + 32, :] = v

    stores = []
    m_load.wait()
    pack(MI, put_mom)
    stores.append(copy(MO, mom_out, sem.at[5]))
    o_load.wait()
    for i in range(parts):
        w_loads[i].wait()
        G[i] = dot_nt(O[...], W[cols * i : cols * i + cols, :]).astype(BF16)
        stores.append(copy(G.at[i], grad_out.at[:, pl.ds(cols * i, cols)], g_sem.at[i]))
        if i == parts - 1:
            u_load.wait()
            pack(UI, put_upd)
            for m in range(32):
                UO[:, 128 * m : 128 * m + 128] = packed[pl.ds(m, 28, stride=32), :]
            stores.append(copy(UO, upd_out, sem.at[6]))
    l_load.wait()
    stores.append(copy(L, lat_out, sem.at[4]))
    for cp in stores:
        cp.wait()


def on_device(tokens, out_grad, proj_weight, momentum, freq_index):
    grad_scale = 1.0 / math.sqrt(TOK * 32)
    any_spec = pl.BlockSpec(memory_space=pl.ANY)
    vmem = pl.BlockSpec(memory_space=pltpu.VMEM)
    dma = pltpu.SemaphoreType.DMA
    full, mom_hb, upd_hb, lat = pl.pallas_call(
        functools.partial(kernel, grad_scale),
        out_shape=(
            jax.ShapeDtypeStruct((32, 2, 112, KV), BF16),
            jax.ShapeDtypeStruct((HB, 2, SIDE, 128), F32),
            jax.ShapeDtypeStruct((HB, 2, SIDE, 128), F32),
            jax.ShapeDtypeStruct((TOK, KV), BF16),
        ),
        in_specs=[any_spec, any_spec, any_spec, any_spec, any_spec, vmem],
        out_specs=(any_spec, vmem, vmem, vmem),
        scratch_shapes=[
            pltpu.VMEM((TOK, WIDE), BF16),
            pltpu.VMEM((WIDE, TOK), BF16),
            pltpu.VMEM((TOK, KV), BF16),
            pltpu.VMEM((32, 2, 112, KV), BF16),
            pltpu.VMEM((4, 8, 64, 256), F32),
            pltpu.VMEM((3, 2, 4, 2, HB, 32, 256), I16),
            pltpu.VMEM((3, 2, 4, 2, 128), F32),
            pltpu.VMEM((3, 2, 4, 2, HB, 32, 256), I16),
            pltpu.VMEM((3, 2, 4, 2, 128), F32),
            pltpu.VMEM((2, 4, 2, HB, 32, 256), F32),
            pltpu.VMEM((4, 2, HB, 64, 256), F32),
            pltpu.VMEM((4, 2, HB, 32, 256), I16),
            pltpu.VMEM((4, 2, 128), F32),
            pltpu.VMEM((4, 2, HB, 32, 256), I16),
            pltpu.VMEM((4, 2, 128), F32),
            pltpu.VMEM((3, 2, HB, 32, 256), I16),
            pltpu.VMEM((3, 2, 1, 128), F32),
            pltpu.VMEM((3, 2, HB, 32, 256), I16),
            pltpu.VMEM((3, 2, 1, 128), F32),
            pltpu.VMEM((4 * HB, 256, 128), BF16),
            pltpu.VMEM((4 * HB, 256, 128), BF16),
            pltpu.VMEM((4 * HB, 64, 128), F32),
            pltpu.VMEM((4, HB, 1, 128), F32),
            pltpu.VMEM((4 * HB, 32, 128), F32),
            pltpu.VMEM((HB, 2, SIDE, 128), F32),
            pltpu.VMEM((4 * HB, 4, 32), jnp.int32),
            pltpu.VMEM((TOK, KV), F32),
            pltpu.VMEM((4, 2, HB, 32, 256), I16),
            pltpu.VMEM((4, 2, 128), F32),
            pltpu.VMEM((4, 2, HB, 32, 256), I16),
            pltpu.VMEM((4, 2, 128), F32),
            dma((9,)),
            dma((4,)),
            dma((31,)),
            dma((31,)),
            dma((31,)),
            dma((31,)),
            dma((3, 2, 4, 2)),
            dma((3, 2, 4, 2)),
            dma((4, 2)),
            dma((4, 2)),
            dma((3, 2, 2)),
            dma((3, 2, 2)),
            dma((3,)),
            dma((3,)),
            dma((4, 2)),
            dma((4, 2)),
            dma((8,)),
        ],
        compiler_params=pltpu.CompilerParams(
            collective_id=0, has_side_effects=True, vmem_limit_bytes=62 << 20
        ),
        cost_estimate=pl.CostEstimate(
            flops=8 * 10**9, bytes_accessed=24 * 10**6, transcendentals=0
        ),
    )(
        tokens,
        out_grad,
        proj_weight.reshape(2, 112, KV),
        momentum.reshape(4 * HB, 32, 128),
        freq_index.transpose(1, 0, 2),
        jnp.asarray(cosine_tables()),
    )
    parts = 4
    cols = WIDE // parts
    grad_in, mom_out, upd, latent = pl.pallas_call(
        finish_kernel,
        out_shape=(
            jax.ShapeDtypeStruct((TOK, WIDE), BF16),
            jax.ShapeDtypeStruct((4 * HB, 32, 128), F32),
            jax.ShapeDtypeStruct((4 * HB, SIDE * SIDE), F32),
            jax.ShapeDtypeStruct((TOK, KV), BF16),
        ),
        in_specs=[any_spec] * 5,
        out_specs=(any_spec,) * 4,
        scratch_shapes=[
            pltpu.VMEM((TOK, KV), BF16),
            pltpu.VMEM((WIDE, KV), BF16),
            pltpu.VMEM((parts, TOK, cols), BF16),
            pltpu.VMEM((HB, 2, SIDE, 128), F32),
            pltpu.VMEM((HB, 2, SIDE, 128), F32),
            pltpu.VMEM((TOK, KV), BF16),
            pltpu.VMEM((4 * HB, 32, 128), F32),
            pltpu.VMEM((28 * 32, 128), F32),
            pltpu.VMEM((4 * HB, SIDE * SIDE), F32),
            dma((parts,)),
            dma((parts,)),
            dma((7,)),
        ],
        compiler_params=pltpu.CompilerParams(vmem_limit_bytes=62 << 20),
        cost_estimate=pl.CostEstimate(
            flops=4 * 10**9, bytes_accessed=16 * 10**6, transcendentals=0
        ),
    )(out_grad, full.reshape(WIDE, KV), mom_hb, upd_hb, lat)
    return latent, grad_in, mom_out.reshape(1, 4 * HB, SIDE * SIDE), upd


def solution(mesh):
    return jax.shard_map(
        on_device,
        mesh=mesh,
        in_specs=(
            P(("group", "fsdp"), None),
            P(("group", "fsdp"), None),
            P("fsdp", None),
            P("group", "fsdp", None),
            P(None, "fsdp", None),
        ),
        out_specs=(
            P(("group", "fsdp"), None),
            P(("group", "fsdp"), None),
            P("group", "fsdp", None),
            P("fsdp", None),
        ),
        check_vma=False,
    )
```
